32 devices in a mesh: kz: 4 (over y, x), gx: 8 (over z, core).
Axes of the slice: x: 2, y: 2, z: 4, core: 2. Of those that a mesh axis runs over, the one named last changes fastest.
Arguments:
- kspace_lines: bfloat16 [16, 4, 32, 2, 512], P(None, 'kz', 'gx'), may hold values from -6 to 6
- acquired_at: int32 [4, 32], P('kz'), may hold values from 0 to 5
- ky_start: int32 [6], replicated, may hold values from -2 to 0, as said below
- kz_start: int32 [6], replicated, may hold values from -1 to 0, as said below
- kernels: bfloat16 [2, 6, 16, 6, 32], replicated, may hold values from -0.3125 to 0.3125
Outputs:
- filled: bfloat16 [2, 512, 16, 8, 96], P(None, 'gx', None, 'kz')
The draws below stay inside these ranges and needn't reach their ends.
Inputs may be any that keep to these rules, and one draw needn't show every extreme that they name: acquired_at[b, a] = 2 ry + rz names the acquired position of the cell, with ky = 3 a + ry and kz = 2 b + rz. `ky_start`: each of -2, -1 and 0 appears exactly twice. `kz_start`: each of -1 and 0 appears exactly three times.
All inputs are finite; a program needn't handle non-finite values.
Results may differ from the reference program's by a relative error of at most 0.0057.
Values may be sent and summed in bfloat16 or wider, within the bound.
A program may use at most 64 MiB of HBM per device.

```python
import math
import jax
import jax.numpy as jnp
from jax import lax

COILS = 16
NX = 512
NZC = 4
NY3 = 32
NZ = 8
NY = 96


def draw_ky_start(key, part):
    return (jax.random.permutation(key, 6) % 3 - 2).astype(jnp.int32)


def draw_kz_start(key, part):
    return (jax.random.permutation(jax.random.fold_in(key, 7), 6) % 2 - 1).astype(jnp.int32)


def place_ends(values, stream_key, least, high):
    longest = values.shape.index(max(values.shape))
    spots = []
    for shift in (0, 1):
        where = [jax.random.randint(jax.random.fold_in(stream_key, axis), (), 0, length) for axis, length in enumerate(values.shape)]
        where[longest] = (where[longest] + shift) % values.shape[longest]
        spots.append(tuple(where))
    return values.at[spots[0]].set(least).at[spots[1]].set(high)


def steps_of(stream_key, shape, cuts, least, top_value):
    loudness = 1.0
    for dim, shards_of in cuts:
        draws = jax.random.uniform(jax.random.fold_in(jax.random.fold_in(stream_key, 6), dim), (shards_of,), jnp.float32, least / len(cuts), top_value / len(cuts))
        loudness = loudness * jnp.repeat(jnp.exp(draws), shape[dim] // shards_of).reshape((-1,) + (1,) * (len(shape) - 1 - dim))
    return loudness


def bell_draw(rng, dims, deviation, most, shards=(), kind=jnp.bfloat16):
    values = deviation * jax.random.normal(rng, dims, jnp.float32)
    if shards:
        values = values * steps_of(rng, dims, shards, -0.22, 0.18)
    return jnp.clip(values, -most, most).astype(kind)


def setup_inputs(seed: int = 0) -> dict:
    keys = jax.random.split(jax.random.key(seed), 6)
    kspace_lines = bell_draw(keys[0], (COILS, NZC, NY3, 2, NX), 1.0, 6.0, ((1, 4), (2, 8)))
    acquired_at = place_ends(jax.random.randint(keys[1], (NZC, NY3), 0, 6), jax.random.fold_in(keys[1], 1), 0, 5).astype(jnp.int32)
    ky_start = draw_ky_start(jax.random.fold_in(keys[5], 71), 0)
    kz_start = draw_kz_start(jax.random.fold_in(keys[5], 71), 0)
    kernels = bell_draw(keys[4], (2, 6, COILS, 6, 2 * COILS), (24 * COILS) ** -0.5, 0.3125)
    return dict(kspace_lines=kspace_lines, acquired_at=acquired_at, ky_start=ky_start, kz_start=kz_start, kernels=kernels)


def readout_matrix(extent):
    wave_index = jnp.arange(extent, dtype=jnp.int32)
    phase_angle = (wave_index[:, None] * wave_index[None, :] % extent).astype(jnp.float32) * (2.0 * math.pi / extent)
    cosine = jnp.cos(phase_angle) / math.sqrt(extent)
    sine_part = jnp.sin(phase_angle) / math.sqrt(extent)
    from_real = jnp.stack([cosine, sine_part], axis=1)
    from_imag = jnp.stack([-sine_part, cosine], axis=1)
    return jnp.stack([from_real, from_imag], axis=0).astype(jnp.bfloat16)

def conjugate_flip(blocks):
    flipped = blocks[:, :, :, ::-1, ::-1]
    return jnp.concatenate([flipped[0:1], -flipped[1:2]], axis=0)

def complex_weights(kernels):
    real_part = kernels[0]
    imag_part = kernels[1]
    to_real = jnp.stack([real_part, -imag_part], axis=3)
    to_imag = jnp.stack([imag_part, real_part], axis=3)
    return jnp.stack([to_real, to_imag], axis=1)

def fill_grid(padded, actual, weights, acquired_at, ky_start, kz_start):
    kz_cells = actual.shape[3]
    ky_cells = actual.shape[4]
    filled = []
    for target in range(6):
        pieces = []
        for kz_point in range(2):
            kz_from = (kz_start[target] + 1 + kz_point).astype(jnp.int32)
            plane_rows = lax.dynamic_slice_in_dim(padded, kz_from, kz_cells, axis=3)
            for ky_point in range(3):
                ky_from = (ky_start[target] + 2 + ky_point).astype(jnp.int32)
                pieces.append(lax.dynamic_slice_in_dim(plane_rows, ky_from, ky_cells, axis=4))
        source = jnp.stack(pieces, axis=0).astype(jnp.float32)
        estimate = jnp.einsum('scpqh,pqxhba->sxcba', weights[target].astype(jnp.float32), source)
        chosen = jnp.where(acquired_at == target, actual.astype(jnp.float32), estimate)
        filled.append(chosen.astype(jnp.bfloat16))
    stacked = jnp.stack(filled, axis=0).reshape((3, 2) + actual.shape)
    reordered = jnp.transpose(stacked, (2, 3, 4, 5, 1, 6, 0))
    return reordered.reshape(actual.shape[0], actual.shape[1], actual.shape[2], 2 * kz_cells, 3 * ky_cells)

def reference(kspace_lines, acquired_at, ky_start, kz_start, kernels):
    spectra = jnp.einsum('cbaqk,qksx->sxcba', kspace_lines.astype(jnp.float32), readout_matrix(NX).astype(jnp.float32)).astype(jnp.bfloat16)
    channels = jnp.concatenate([spectra, conjugate_flip(spectra)], axis=2)
    padded = jnp.pad(channels, ((0, 0), (0, 0), (0, 0), (1, 1), (2, 2)))
    weights = complex_weights(kernels)
    block_width = math.gcd(NX, 16)
    groups = NX // block_width

    def split_x(values):
        return jnp.moveaxis(values.reshape((2, groups, block_width) + values.shape[2:]), 1, 0)

    def one_group(operands):
        return fill_grid(operands[0], operands[1], weights, acquired_at, ky_start, kz_start)
    result = lax.map(one_group, (split_x(padded), split_x(spectra)))
    return jnp.moveaxis(result, 0, 1).reshape(2, NX, COILS, NZ, NY)
```

```python
import functools
import math

import jax
import jax.numpy as jnp
import ml_dtypes
import numpy as np
from jax import lax
from jax.experimental import pallas as pl
from jax.experimental.pallas import tpu as pltpu
from jax.sharding import PartitionSpec as P

BF16 = ml_dtypes.bfloat16
MESH = pl.DeviceIdType.MESH
GROUP = 4
EDGE = 4
LIMIT = 50 * 1024 * 1024


def readout_table(extent):
    index = np.arange(extent)
    angle = (index[:, None] * index[None, :] % extent) * (2.0 * math.pi / extent)
    return np.concatenate([np.cos(angle), np.sin(angle)], axis=1).astype(np.float64) / math.sqrt(extent)


def line_order(coils, cells):
    order = np.zeros((2, cells, 2, coils, coils, cells, 2), np.float32)
    for c in range(coils):
        for a in range(cells):
            order[0, a, 0, c, c, a, 0] = 1
            order[0, a, 1, c, c, a, 1] = 1
            order[1, a, 0, c, c, a, 1] = -1
            order[1, a, 1, c, c, a, 0] = 1
    return order.reshape(4 * cells * coils, 2 * coils * cells).astype(BF16)


def slab_order(values):
    order = np.zeros((GROUP, GROUP, values, GROUP, GROUP, values), np.float32)
    for b in range(GROUP):
        for a in range(GROUP):
            for v in range(values):
                order[b, a, v, a, b, v] = 1
    return order.reshape(GROUP * GROUP * values, -1).astype(BF16)


def weight_lanes(coils):
    lanes = np.zeros((2, 2, coils, 2, 2, GROUP, 2, coils), np.float32)
    for v in range(2):
        sign = -1 if v else 1
        for c in range(coils):
            lanes[0, v, c, 0, v, :, 0, c] = 1
            lanes[1, v, c, 0, v, :, 1, c] = -sign
            lanes[1, v, c, 1, v, :, 0, c] = 1
            lanes[0, v, c, 1, v, :, 1, c] = sign
    return lanes.reshape(2, 2 * coils, -1).astype(BF16)


def row_order(coils):
    values = 2 * coils
    order = np.zeros((4, values, 2, 7 * values), np.float32)
    for n in range(values):
        for rz in range(2):
            for ry in range(3):
                order[ry, n, rz, (ry * 2 + rz) * values + n] = 1
            order[3, n, rz, 6 * values + n] = 1
    return order.reshape(8 * values, 7 * values).astype(BF16)


def lane_order(cells, width):
    each = 128 // cells
    order = np.zeros((3, each, cells, each, width), np.float32)
    for ry in range(3):
        for x in range(each):
            for a in range(cells):
                order[ry, x, a, x, 3 * a + ry] = 1
    return order.reshape(3 * 128, each * width).astype(BF16)


def nt(left, right):
    return lax.dot_general(left, right, (((1,), (1,)), ((), ())), preferred_element_type=jnp.float32)


def gather_kernel(nkz, ngx, table, lines, order, planes, spectra, send_x, recv_x, send_z, recv_z):
    b, g = lax.axis_index("kz"), lax.axis_index("gx")
    barrier = pltpu.get_barrier_semaphore()
    for k in range(1, ngx):
        pl.semaphore_signal(barrier, inc=1, device_id=(b, lax.rem(g + k, ngx)), device_id_type=MESH)
    for j in range(1, nkz):
        pl.semaphore_signal(barrier, inc=1, device_id=(lax.rem(b + j, nkz), g), device_id_type=MESH)

    count = lines.shape[0]
    both = jnp.dot(order[...], lines[...], preferred_element_type=jnp.float32).astype(jnp.bfloat16)
    right = jnp.concatenate([both[:count], both[count:]], axis=1)
    values = nt(table[...], right).astype(jnp.bfloat16)
    spectra[...] = values.reshape(spectra.shape)
    planes[b, g] = spectra[g]

    pl.semaphore_wait(barrier, ngx + nkz - 2)
    along_x, along_z = {}, {}
    for k in range(1, ngx):
        to = lax.rem(g + k, ngx)
        along_x[k] = pltpu.make_async_remote_copy(
            src_ref=spectra.at[to], dst_ref=planes.at[b, g], send_sem=send_x.at[k],
            recv_sem=recv_x.at[k], device_id=(b, to), device_id_type=MESH)
        along_x[k].start()
    for k in range(ngx):
        if k:
            along_x[k].wait_recv()
        source = lax.rem(g + ngx - k, ngx)
        for j in range(1, nkz):
            along_z[j, k] = pltpu.make_async_remote_copy(
                src_ref=planes.at[b, source], dst_ref=planes.at[b, source], send_sem=send_z.at[j, k],
                recv_sem=recv_z.at[j, k], device_id=(lax.rem(b + j, nkz), g), device_id_type=MESH)
            along_z[j, k].start()
    for copy in along_z.values():
        copy.wait_recv()
    for copy in list(along_x.values()) + list(along_z.values()):
        copy.wait_send()


def fill_kernel(nkz, ky_start, kz_start, planes, parts, acquired, to_slabs, to_lanes, to_rows, to_ky,
                out, near, far, natural, weights):
    b = lax.axis_index("kz")
    _, ngx, xs, lanes = planes.shape
    cells = ngx * GROUP
    pitch = cells + 2 * EDGE
    sets = nkz // GROUP
    coils = parts.shape[3]
    values = 2 * coils
    f32, bf16 = jnp.float32, jnp.bfloat16

    terms = (
        jnp.dot(parts[0].reshape(36 * coils, values), to_lanes[0], preferred_element_type=f32)
        + jnp.dot(parts[1].reshape(36 * coils, values), to_lanes[1], preferred_element_type=f32)
    )
    lane = lax.broadcasted_iota(jnp.int32, (coils, 128), 1)
    slab = lane // values
    for t in range(6):
        for v in range(2):
            for part in range(sets):
                cell = slab + part * GROUP
                if v:
                    cell = nkz - 1 - cell
                point = cell - b - kz_start[t]
                for s in range(2):
                    column = (s * 2 + v) * 128
                    rows = []
                    for i in range(3):
                        at = (t * 6 + i) * coils
                        first = terms[at : at + coils, column : column + 128]
                        second = terms[at + 3 * coils : at + 4 * coils, column : column + 128]
                        rows.append(jnp.where(point == 0, first, jnp.where(point == 1, second, 0.0)))
                    for d in range(-2, 3):
                        total = jnp.zeros((coils, 128), f32)
                        for i in range(3):
                            if -2 <= d - i <= 0:
                                here = jnp.full((coils, 128), ky_start[t], jnp.int32) == d - i
                                total = jnp.where(here, rows[i], total)
                        where = ((v * 5 + d + 2) * sets + part) * 128
                        natural[(t * 2 + s) * coils : (t * 2 + s + 1) * coils, where : where + 128] = total.astype(bf16)
    natural[12 * coils :, :] = jnp.zeros((values, natural.shape[1]), bf16)
    row = lax.broadcasted_iota(jnp.int32, (values, 128), 0)
    wide = lax.broadcasted_iota(jnp.int32, (values, 128), 1)
    for part in range(sets):
        same = (b - part * GROUP) * values + row == wide
        where = (2 * sets + part) * 128
        natural[12 * coils :, where : where + 128] = jnp.where(same, 1.0, 0.0).astype(bf16)
    weights[...] = jnp.dot(to_rows[...], natural[...], preferred_element_type=f32).astype(bf16)

    for x in range(sets * xs):
        for buffer in (near, far):
            buffer[x * pitch : x * pitch + EDGE, :] = jnp.zeros((EDGE, buffer.shape[1]), f32)
            buffer[(x + 1) * pitch - EDGE : (x + 1) * pitch, :] = jnp.zeros((EDGE, buffer.shape[1]), f32)
    for part in range(sets):
        for g in range(ngx):
            block = jnp.concatenate([planes[part * GROUP + n, g] for n in range(GROUP)], axis=1)
            turned = jnp.dot(block, to_slabs[...], preferred_element_type=f32)
            for n in range(GROUP):
                a = g * GROUP + n
                piece = turned[:, n * 128 : (n + 1) * 128]
                base = part * xs * pitch + EDGE
                near[pl.ds(base + a, xs, stride=pitch), :] = piece
                far[pl.ds(base + cells - 1 - a, xs, stride=pitch), :] = piece

    each = 128 // cells
    width = to_ky.shape[1] // each
    step = 2 * each
    odd = lax.broadcasted_iota(jnp.int32, (2 * values, 2 * 128), 0) % 2
    for start in range(0, xs, step):
        pieces = []
        for buffer in (near, far):
            for d in range(-2, 3):
                for part in range(sets):
                    rows = [(part * xs + x) * pitch + EDGE + d for x in range(start, start + step)]
                    pieces.append(jnp.concatenate([buffer[r : r + cells, :] for r in rows], axis=0).astype(bf16))
        result = nt(weights[...], jnp.concatenate(pieces, axis=1))
        actual = result[6 * values :]
        chosen = [
            jnp.where(acquired[...] == odd + 2 * ry, actual, result[ry * 2 * values : (ry + 1) * 2 * values]).astype(bf16)
            for ry in range(3)
        ]
        for half in range(2):
            line = jnp.concatenate([c[:, half * 128 : (half + 1) * 128] for c in chosen], axis=1)
            spread = jnp.dot(line, to_ky[...], preferred_element_type=f32).astype(bf16)
            for n in range(each):
                x = start + half * each + n
                for s in range(2):
                    out[s * xs + x] = spread[s * values : (s + 1) * values, n * width : n * width + 3 * cells]


def local(kspace_lines, acquired_at, ky_start, kz_start, kernels):
    nkz, ngx = lax.axis_size("kz"), lax.axis_size("gx")
    coils, _, own, _, extent = kspace_lines.shape
    xs, cells = extent // ngx, ngx * own
    assert own == GROUP and nkz % GROUP == 0 and 2 * coils * GROUP == 128 and 128 % cells == 0
    vmem = pl.BlockSpec(memory_space=pltpu.VMEM)
    smem = pl.BlockSpec(memory_space=pltpu.SMEM)
    table = jnp.asarray(readout_table(extent).astype(BF16))
    planes = pl.pallas_call(
        functools.partial(gather_kernel, nkz, ngx),
        out_shape=jax.ShapeDtypeStruct((nkz, ngx, xs, 128), jnp.bfloat16),
        in_specs=[vmem] * 3,
        out_specs=vmem,
        scratch_shapes=[
            pltpu.VMEM((ngx, xs, 128), jnp.bfloat16),
            pltpu.SemaphoreType.DMA((ngx,)),
            pltpu.SemaphoreType.DMA((ngx,)),
            pltpu.SemaphoreType.DMA((nkz, ngx)),
            pltpu.SemaphoreType.DMA((nkz, ngx)),
        ],
        compiler_params=pltpu.CompilerParams(
            collective_id=0, has_side_effects=True, vmem_limit_bytes=LIMIT),
    )(table, kspace_lines.reshape(coils * own * 2, extent), jnp.asarray(line_order(coils, own)))

    each = 128 // cells
    width = -(-3 * cells // 128) * 128
    sets = nkz // GROUP
    taps = 10 * 128 * sets
    pitch = cells + 2 * EDGE
    filled = pl.pallas_call(
        functools.partial(fill_kernel, nkz),
        out_shape=jax.ShapeDtypeStruct((2 * xs, 2 * coils, 3 * cells), jnp.bfloat16),
        in_specs=[smem, smem] + [vmem] * 7,
        out_specs=vmem,
        scratch_shapes=[
            pltpu.VMEM((sets * xs * pitch, 128), jnp.float32),
            pltpu.VMEM((sets * xs * pitch, 128), jnp.float32),
            pltpu.VMEM((14 * coils, taps), jnp.bfloat16),
            pltpu.VMEM((16 * coils, taps), jnp.bfloat16),
        ],
        compiler_params=pltpu.CompilerParams(vmem_limit_bytes=LIMIT),
    )(
        ky_start, kz_start, planes, jnp.transpose(kernels, (0, 1, 3, 2, 4)),
        jnp.tile(acquired_at, (1, 2 * each)), jnp.asarray(slab_order(2 * coils)),
        jnp.asarray(weight_lanes(coils)), jnp.asarray(row_order(coils)), jnp.asarray(lane_order(cells, width)),
    )
    return filled.reshape(2, xs, coils, 2, 3 * cells)


def solution(mesh):
    placed = (P(None, "kz", "gx", None, None), P("kz", None), P(), P(), P())
    return jax.shard_map(
        local,
        mesh=mesh,
        in_specs=placed,
        out_specs=P(None, "gx", None, "kz", None),
        check_vma=False,
    )
```

```python
import functools
import math

import jax
import jax.numpy as jnp
import ml_dtypes
import numpy as np
from jax import lax
from jax.experimental import pallas as pl
from jax.experimental.pallas import tpu as pltpu
from jax.sharding import PartitionSpec as P

BF16 = ml_dtypes.bfloat16
MESH = pl.DeviceIdType.MESH
GROUP = 4
EDGE = 4
LIMIT = 50 * 1024 * 1024


def readout_table(extent):
    index = np.arange(extent)
    angle = (index[:, None] * index[None, :] % extent) * (2.0 * math.pi / extent)
    return np.concatenate([np.cos(angle), np.sin(angle)], axis=1).astype(np.float64) / math.sqrt(extent)


def line_order(coils, cells):
    order = np.zeros((2, cells, 2, coils, coils, cells, 2), np.float32)
    for c in range(coils):
        for a in range(cells):
            order[0, a, 0, c, c, a, 0] = 1
            order[0, a, 1, c, c, a, 1] = 1
            order[1, a, 0, c, c, a, 1] = -1
            order[1, a, 1, c, c, a, 0] = 1
    return order.reshape(4 * cells * coils, 2 * coils * cells).astype(BF16)


def slab_order(values):
    order = np.zeros((GROUP, GROUP, values, GROUP, GROUP, values), np.float32)
    for b in range(GROUP):
        for a in range(GROUP):
            for v in range(values):
                order[b, a, v, a, b, v] = 1
    return order.reshape(GROUP * GROUP * values, -1).astype(BF16)


def weight_lanes(coils):
    lanes = np.zeros((2, 2, coils, 2, 2, GROUP, 2, coils), np.float32)
    for v in range(2):
        sign = -1 if v else 1
        for c in range(coils):
            lanes[0, v, c, 0, v, :, 0, c] = 1
            lanes[1, v, c, 0, v, :, 1, c] = -sign
            lanes[1, v, c, 1, v, :, 0, c] = 1
            lanes[0, v, c, 1, v, :, 1, c] = sign
    return lanes.reshape(2, 2 * coils, -1).astype(BF16)


def row_order(coils):
    values = 2 * coils
    order = np.zeros((4, values, 2, 7 * values), np.float32)
    for n in range(values):
        for rz in range(2):
            for ry in range(3):
                order[ry, n, rz, (ry * 2 + rz) * values + n] = 1
            order[3, n, rz, 6 * values + n] = 1
    return order.reshape(8 * values, 7 * values).astype(BF16)


def lane_order(cells, width):
    each = 128 // cells
    order = np.zeros((3, each, cells, each, width), np.float32)
    for ry in range(3):
        for x in range(each):
            for a in range(cells):
                order[ry, x, a, x, 3 * a + ry] = 1
    return order.reshape(3 * 128, each * width).astype(BF16)


def nt(left, right):
    return lax.dot_general(left, right, (((1,), (1,)), ((), ())), preferred_element_type=jnp.float32)


def gather_kernel(nkz, ngx, ky_start, kz_start, table_hbm, lines, order, parts, to_slabs, to_lanes, to_rows,
                  near, far, weights, table, planes, spectra, natural, load, send_x, recv_x, send_z, recv_z):
    b, g = lax.axis_index("kz"), lax.axis_index("gx")
    barrier = pltpu.get_barrier_semaphore()
    for k in range(1, ngx):
        pl.semaphore_signal(barrier, inc=1, device_id=(b, lax.rem(g + k, ngx)), device_id_type=MESH)
    for j in range(1, nkz):
        pl.semaphore_signal(barrier, inc=1, device_id=(lax.rem(b + j, nkz), g), device_id_type=MESH)
    loading = pltpu.make_async_copy(table_hbm, table, load)
    loading.start()

    f32, bf16 = jnp.float32, jnp.bfloat16
    sets = nkz // GROUP
    coils = parts.shape[3]
    values = 2 * coils
    cells = ngx * GROUP
    pitch = cells + 2 * EDGE
    xs = spectra.shape[1]

    count = values * GROUP
    both = jnp.dot(order[...], lines[...].reshape(count, table.shape[0]), preferred_element_type=f32).astype(bf16)
    right = jnp.concatenate([both[:count], both[count:]], axis=1)
    terms = (
        jnp.dot(parts[0].reshape(36 * coils, values), to_lanes[0], preferred_element_type=f32)
        + jnp.dot(parts[1].reshape(36 * coils, values), to_lanes[1], preferred_element_type=f32)
    )
    loading.wait()
    spectra[...] = nt(table[...], right).astype(bf16).reshape(spectra.shape)
    planes[b, g] = spectra[g]

    pl.semaphore_wait(barrier, ngx + nkz - 2)
    along_x, along_z = {}, {}

    def forward(k):
        source = lax.rem(g + ngx - k, ngx)
        for j in range(1, nkz):
            along_z[j, k] = pltpu.make_async_remote_copy(
                src_ref=planes.at[b, source], dst_ref=planes.at[b, source], send_sem=send_z.at[j, k],
                recv_sem=recv_z.at[j, k], device_id=(lax.rem(b + j, nkz), g), device_id_type=MESH)
            along_z[j, k].start()

    for k in range(1, ngx):
        to = lax.rem(g + k, ngx)
        along_x[k] = pltpu.make_async_remote_copy(
            src_ref=spectra.at[to], dst_ref=planes.at[b, g], send_sem=send_x.at[k],
            recv_sem=recv_x.at[k], device_id=(b, to), device_id_type=MESH)
        along_x[k].start()
    forward(0)

    lane = lax.broadcasted_iota(jnp.int32, (coils, 128), 1)
    slab = lane // values

    def place(t):
        here = {n: jnp.full((coils, 128), ky_start[t], jnp.int32) == n for n in (-2, -1, 0)}
        for v in range(2):
            for part in range(sets):
                cell = slab + part * GROUP
                if v:
                    cell = nkz - 1 - cell
                point = cell - b - kz_start[t]
                for s in range(2):
                    column = (s * 2 + v) * 128
                    rows = []
                    for i in range(3):
                        at = (t * 6 + i) * coils
                        first = terms[at : at + coils, column : column + 128]
                        second = terms[at + 3 * coils : at + 4 * coils, column : column + 128]
                        rows.append(jnp.where(point == 0, first, jnp.where(point == 1, second, 0.0)))
                    for d in range(-2, 3):
                        total = jnp.zeros((coils, 128), f32)
                        for i in range(3):
                            if -2 <= d - i <= 0:
                                total = jnp.where(here[d - i], rows[i], total)
                        where = ((v * 5 + d + 2) * sets + part) * 128
                        natural[(t * 2 + s) * coils : (t * 2 + s + 1) * coils, where : where + 128] = total.astype(bf16)

    def place_rest():
        natural[12 * coils :, :] = jnp.zeros((values, natural.shape[1]), bf16)
        row = lax.broadcasted_iota(jnp.int32, (values, 128), 0)
        wide = lax.broadcasted_iota(jnp.int32, (values, 128), 1)
        for part in range(sets):
            same = (b - part * GROUP) * values + row == wide
            where = (2 * sets + part) * 128
            natural[12 * coils :, where : where + 128] = jnp.where(same, 1.0, 0.0).astype(bf16)
        for x in range(sets * xs):
            for buffer in (near, far):
                buffer[x * pitch : x * pitch + EDGE, :] = jnp.zeros((EDGE, 128), f32)
                buffer[(x + 1) * pitch - EDGE : (x + 1) * pitch, :] = jnp.zeros((EDGE, 128), f32)

    work = [functools.partial(place, t) for t in range(6)] + [place_rest]
    for k in range(1, ngx):
        along_x[k].wait_recv()
        forward(k)
        if work:
            work.pop(0)()
    weights[...] = jnp.dot(to_rows[...], natural[...], preferred_element_type=f32).astype(bf16)

    for k in range(ngx):
        for j in range(1, nkz):
            along_z[j, k].wait_recv()
        source = lax.rem(g + ngx - k, ngx)
        for part in range(sets):
            block = jnp.concatenate([planes[part * GROUP + n, source] for n in range(GROUP)], axis=1)
            turned = jnp.dot(block, to_slabs[...], preferred_element_type=f32)
            for n in range(GROUP):
                piece = turned[:, n * 128 : (n + 1) * 128]
                base = part * xs * pitch + EDGE
                near[pl.ds(base + source * GROUP + n, xs, stride=pitch), :] = piece
                far[pl.ds(base + cells - 1 - n - source * GROUP, xs, stride=pitch), :] = piece
    for copy in list(along_x.values()) + list(along_z.values()):
        copy.wait_send()


def fill_kernel(sets, xs, near, far, weights, acquired, to_ky, out):
    cells = acquired.shape[1]
    values = weights.shape[0] // 8
    pitch = cells + 2 * EDGE
    f32, bf16 = jnp.float32, jnp.bfloat16
    each = 128 // cells
    width = to_ky.shape[1] // each
    step = 2 * each
    odd = lax.broadcasted_iota(jnp.int32, (2 * values, 2 * 128), 0) % 2
    position = jnp.concatenate([acquired[...]] * step, axis=1) - odd
    for start in range(0, xs, step):
        pieces = []
        for buffer in (near, far):
            for d in range(-2, 3):
                for part in range(sets):
                    rows = [(part * xs + x) * pitch + EDGE + d for x in range(start, start + step)]
                    pieces.append(jnp.concatenate([buffer[r : r + cells, :] for r in rows], axis=0).astype(bf16))
        result = nt(weights[...], jnp.concatenate(pieces, axis=1))
        actual = result[6 * values :]
        chosen = [
            jnp.where(position == 2 * ry, actual, result[ry * 2 * values : (ry + 1) * 2 * values]).astype(bf16)
            for ry in range(3)
        ]
        for half in range(2):
            line = jnp.concatenate([c[:, half * 128 : (half + 1) * 128] for c in chosen], axis=1)
            spread = jnp.dot(line, to_ky[...], preferred_element_type=f32).astype(bf16)
            for n in range(each):
                x = start + half * each + n
                for s in range(2):
                    out[s * xs + x] = spread[s * values : (s + 1) * values, n * width : n * width + 3 * cells]


def local(kspace_lines, acquired_at, ky_start, kz_start, kernels):
    nkz, ngx = lax.axis_size("kz"), lax.axis_size("gx")
    coils, _, own, _, extent = kspace_lines.shape
    xs, cells = extent // ngx, ngx * own
    assert own == GROUP and nkz % GROUP == 0 and 2 * coils * GROUP == 128 and 128 % cells == 0
    vmem = pl.BlockSpec(memory_space=pltpu.VMEM)
    smem = pl.BlockSpec(memory_space=pltpu.SMEM)
    table = jnp.asarray(readout_table(extent).astype(BF16))
    each = 128 // cells
    width = -(-3 * cells // 128) * 128
    sets = nkz // GROUP
    taps = 10 * 128 * sets
    pitch = cells + 2 * EDGE
    lattice = jax.ShapeDtypeStruct((sets * xs * pitch, 128), jnp.float32)
    near, far, weights = pl.pallas_call(
        functools.partial(gather_kernel, nkz, ngx),
        out_shape=(lattice, lattice, jax.ShapeDtypeStruct((16 * coils, taps), jnp.bfloat16)),
        in_specs=[smem, smem, pl.BlockSpec(memory_space=pl.ANY)] + [vmem] * 6,
        out_specs=(vmem, vmem, vmem),
        scratch_shapes=[
            pltpu.VMEM((extent, 2 * extent), jnp.bfloat16),
            pltpu.VMEM((nkz, ngx, xs, 128), jnp.bfloat16),
            pltpu.VMEM((ngx, xs, 128), jnp.bfloat16),
            pltpu.VMEM((14 * coils, taps), jnp.bfloat16),
            pltpu.SemaphoreType.DMA,
            pltpu.SemaphoreType.DMA((ngx,)),
            pltpu.SemaphoreType.DMA((ngx,)),
            pltpu.SemaphoreType.DMA((nkz, ngx)),
            pltpu.SemaphoreType.DMA((nkz, ngx)),
        ],
        compiler_params=pltpu.CompilerParams(
            collective_id=0, has_side_effects=True, vmem_limit_bytes=LIMIT),
    )(
        ky_start, kz_start, table, kspace_lines, jnp.asarray(line_order(coils, own)),
        jnp.transpose(kernels, (0, 1, 3, 2, 4)), jnp.asarray(slab_order(2 * coils)),
        jnp.asarray(weight_lanes(coils)), jnp.asarray(row_order(coils)),
    )
    filled = pl.pallas_call(
        functools.partial(fill_kernel, sets, xs),
        out_shape=jax.ShapeDtypeStruct((2 * xs, 2 * coils, 3 * cells), jnp.bfloat16),
        in_specs=[vmem] * 5,
        out_specs=vmem,
        compiler_params=pltpu.CompilerParams(vmem_limit_bytes=LIMIT),
    )(near, far, weights, acquired_at, jnp.asarray(lane_order(cells, width)))
    return filled.reshape(2, xs, coils, 2, 3 * cells)


def solution(mesh):
    placed = (P(None, "kz", "gx", None, None), P("kz", None), P(), P(), P())
    return jax.shard_map(
        local,
        mesh=mesh,
        in_specs=placed,
        out_specs=P(None, "gx", None, "kz", None),
        check_vma=False,
    )
```

```python
import functools
import math

import jax
import jax.numpy as jnp
import ml_dtypes
import numpy as np
from jax import lax
from jax.experimental import pallas as pl
from jax.experimental.pallas import tpu as pltpu
from jax.sharding import PartitionSpec as P

BF16 = ml_dtypes.bfloat16
MESH = pl.DeviceIdType.MESH
GROUP = 4
EDGE = 4
LIMIT = 60 * 1024 * 1024


def readout_table(extent):
    index = np.arange(extent)
    angle = (index[:, None] * index[None, :] % extent) * (2.0 * math.pi / extent)
    return np.concatenate([np.cos(angle), np.sin(angle)], axis=1).astype(np.float64) / math.sqrt(extent)


def line_order(coils, cells):
    order = np.zeros((2, cells, 2, coils, coils, cells, 2), np.float32)
    for c in range(coils):
        for a in range(cells):
            order[0, a, 0, c, c, a, 0] = 1
            order[0, a, 1, c, c, a, 1] = 1
            order[1, a, 0, c, c, a, 1] = -1
            order[1, a, 1, c, c, a, 0] = 1
    return order.reshape(4 * cells * coils, 2 * coils * cells).astype(BF16)


def slab_order(values):
    order = np.zeros((GROUP, GROUP, values, GROUP, GROUP, values), np.float32)
    for b in range(GROUP):
        for a in range(GROUP):
            for v in range(values):
                order[b, a, v, a, b, v] = 1
    return order.reshape(GROUP * GROUP * values, -1).astype(BF16)


def weight_lanes(coils):
    lanes = np.zeros((2, 2, coils, 2, 2, GROUP, 2, coils), np.float32)
    for v in range(2):
        sign = -1 if v else 1
        for c in range(coils):
            lanes[0, v, c, 0, v, :, 0, c] = 1
            lanes[1, v, c, 0, v, :, 1, c] = -sign
            lanes[1, v, c, 1, v, :, 0, c] = 1
            lanes[0, v, c, 1, v, :, 1, c] = sign
    return lanes.reshape(2, 2 * coils, -1).astype(BF16)


def row_order(coils):
    values = 2 * coils
    order = np.zeros((4, values, 2, 7 * values), np.float32)
    for n in range(values):
        for rz in range(2):
            for ry in range(3):
                order[ry, n, rz, (ry * 2 + rz) * values + n] = 1
            order[3, n, rz, 6 * values + n] = 1
    return order.reshape(8 * values, 7 * values).astype(BF16)


def lane_order(cells, width):
    each = 128 // cells
    order = np.zeros((3, each, cells, each, width), np.float32)
    for ry in range(3):
        for x in range(each):
            for a in range(cells):
                order[ry, x, a, x, 3 * a + ry] = 1
    return order.reshape(3 * 128, each * width).astype(BF16)


def nt(left, right):
    return lax.dot_general(left, right, (((1,), (1,)), ((), ())), preferred_element_type=jnp.float32)


def kernel(nkz, ngx, *refs):
    sources, out, held = refs[:11], refs[11], refs[12:23]
    lines, order, table, parts, to_lanes, ky_start, kz_start, to_rows, to_slabs, acquired, to_ky = held
    near, far, weights, planes, spectra, natural, chosen, load, send_x, recv_x, send_z, recv_z = refs[23:]
    b, g = lax.axis_index("kz"), lax.axis_index("gx")
    barrier = pltpu.get_barrier_semaphore()
    for k in range(1, ngx):
        pl.semaphore_signal(barrier, inc=1, device_id=(b, lax.rem(g + k, ngx)), device_id_type=MESH)
    for j in range(1, nkz):
        pl.semaphore_signal(barrier, inc=1, device_id=(lax.rem(b + j, nkz), g), device_id_type=MESH)
    loading = [pltpu.make_async_copy(*pair, load.at[n]) for n, pair in enumerate(zip(sources, held))]
    for copy in loading:
        copy.start()

    f32, bf16 = jnp.float32, jnp.bfloat16
    sets = nkz // GROUP
    coils = parts.shape[3]
    values = 2 * coils
    cells = ngx * GROUP
    pitch = cells + 2 * EDGE
    xs = spectra.shape[1]

    count = values * GROUP
    for copy in loading[:2]:
        copy.wait()
    both = jnp.dot(order[...], lines[...].reshape(count, table.shape[0]), preferred_element_type=f32).astype(bf16)
    right = jnp.concatenate([both[:count], both[count:]], axis=1)
    for copy in loading[2:]:
        copy.wait()
    spectra[...] = nt(table[...], right).astype(bf16).reshape(spectra.shape)
    planes[b, g] = spectra[g]
    terms = (
        jnp.dot(parts[0].reshape(36 * coils, values), to_lanes[0], preferred_element_type=f32)
        + jnp.dot(parts[1].reshape(36 * coils, values), to_lanes[1], preferred_element_type=f32)
    )
    pl.semaphore_wait(barrier, ngx + nkz - 2)
    along_x, along_z = {}, {}

    def forward(k):
        source = lax.rem(g + ngx - k, ngx)
        for j in range(1, nkz):
            along_z[j, k] = pltpu.make_async_remote_copy(
                src_ref=planes.at[b, source], dst_ref=planes.at[b, source], send_sem=send_z.at[j, k],
                recv_sem=recv_z.at[j, k], device_id=(lax.rem(b + j, nkz), g), device_id_type=MESH)
            along_z[j, k].start()

    for k in range(1, ngx):
        to = lax.rem(g + k, ngx)
        along_x[k] = pltpu.make_async_remote_copy(
            src_ref=spectra.at[to], dst_ref=planes.at[b, g], send_sem=send_x.at[k],
            recv_sem=recv_x.at[k], device_id=(b, to), device_id_type=MESH)
        along_x[k].start()
    forward(0)

    lane = lax.broadcasted_iota(jnp.int32, (coils, 128), 1)
    slab = lane // values

    def place(t):
        here = {n: jnp.full((coils, 128), ky_start[t], jnp.int32) == n for n in (-2, -1, 0)}
        for v in range(2):
            for part in range(sets):
                cell = slab + part * GROUP
                if v:
                    cell = nkz - 1 - cell
                point = cell - b - kz_start[t]
                for s in range(2):
                    column = (s * 2 + v) * 128
                    rows = []
                    for i in range(3):
                        at = (t * 6 + i) * coils
                        first = terms[at : at + coils, column : column + 128]
                        second = terms[at + 3 * coils : at + 4 * coils, column : column + 128]
                        rows.append(jnp.where(point == 0, first, jnp.where(point == 1, second, 0.0)))
                    for d in range(-2, 3):
                        total = jnp.zeros((coils, 128), f32)
                        for i in range(3):
                            if -2 <= d - i <= 0:
                                total = jnp.where(here[d - i], rows[i], total)
                        where = ((v * 5 + d + 2) * sets + part) * 128
                        natural[(t * 2 + s) * coils : (t * 2 + s + 1) * coils, where : where + 128] = total.astype(bf16)

    def place_rest():
        natural[12 * coils :, :] = jnp.zeros((values, natural.shape[1]), bf16)
        row = lax.broadcasted_iota(jnp.int32, (values, 128), 0)
        wide = lax.broadcasted_iota(jnp.int32, (values, 128), 1)
        for part in range(sets):
            same = (b - part * GROUP) * values + row == wide
            where = (2 * sets + part) * 128
            natural[12 * coils :, where : where + 128] = jnp.where(same, 1.0, 0.0).astype(bf16)
        for x in range(sets * xs):
            for buffer in (near, far):
                buffer[x * pitch : x * pitch + EDGE, :] = jnp.zeros((EDGE, 128), f32)
                buffer[(x + 1) * pitch - EDGE : (x + 1) * pitch, :] = jnp.zeros((EDGE, 128), f32)

    work = [functools.partial(place, t) for t in range(6)] + [place_rest]
    for k in range(1, ngx):
        along_x[k].wait_recv()
        forward(k)
        if work:
            work.pop(0)()
    weights[...] = jnp.dot(to_rows[...], natural[...], preferred_element_type=f32).astype(bf16)

    for k in range(ngx):
        for j in range(1, nkz):
            along_z[j, k].wait_recv()
        source = lax.rem(g + ngx - k, ngx)
        for part in range(sets):
            block = jnp.concatenate([planes[part * GROUP + n, source] for n in range(GROUP)], axis=1)
            turned = jnp.dot(block, to_slabs[...], preferred_element_type=f32)
            for n in range(GROUP):
                piece = turned[:, n * 128 : (n + 1) * 128]
                base = part * xs * pitch + EDGE
                near[pl.ds(base + source * GROUP + n, xs, stride=pitch), :] = piece
                far[pl.ds(base + cells - 1 - n - source * GROUP, xs, stride=pitch), :] = piece

    each = 128 // cells
    width = to_ky.shape[1] // each
    step = 2 * each
    odd = lax.broadcasted_iota(jnp.int32, (2 * values, 2 * 128), 0) % 2
    position = jnp.concatenate([acquired[...]] * step, axis=1) - odd
    for start in range(0, xs, step):
        pieces = []
        for buffer in (near, far):
            for d in range(-2, 3):
                for part in range(sets):
                    rows = [(part * xs + x) * pitch + EDGE + d for x in range(start, start + step)]
                    pieces.append(jnp.concatenate([buffer[r : r + cells, :] for r in rows], axis=0).astype(bf16))
        result = nt(weights[...], jnp.concatenate(pieces, axis=1))
        actual = result[6 * values :]
        for ry in range(3):
            estimate = result[ry * 2 * values : (ry + 1) * 2 * values]
            picked = jnp.where(position == 2 * ry, actual, estimate).astype(bf16)
            for half in range(2):
                at = (start // each + half) * 2 * values
                chosen[at : at + 2 * values, ry * 128 : (ry + 1) * 128] = picked[:, half * 128 : (half + 1) * 128]
    batch = chosen.shape[0] // 2
    for at in range(0, 2 * batch, batch):
        spread = jnp.dot(chosen[at : at + batch, :], to_ky[...], preferred_element_type=f32).astype(bf16)
        for row in range(0, batch, 2 * values):
            for n in range(each):
                x = (at + row) // (2 * values) * each + n
                for s in range(2):
                    first = row + s * values
                    out[s * xs + x] = spread[first : first + values, n * width : n * width + 3 * cells]
    for copy in list(along_x.values()) + list(along_z.values()):
        copy.wait_send()


def local(kspace_lines, acquired_at, ky_start, kz_start, kernels):
    nkz, ngx = lax.axis_size("kz"), lax.axis_size("gx")
    coils, _, own, _, extent = kspace_lines.shape
    xs, cells = extent // ngx, ngx * own
    assert own == GROUP and nkz % GROUP == 0 and 2 * coils * GROUP == 128 and 128 % cells == 0
    each = 128 // cells
    width = -(-3 * cells // 128) * 128
    sets = nkz // GROUP
    taps = 10 * 128 * sets
    lattice = pltpu.VMEM((sets * xs * (cells + 2 * EDGE), 128), jnp.float32)
    operands = [
        kspace_lines,
        jnp.asarray(line_order(coils, own)),
        jnp.asarray(readout_table(extent).astype(BF16)),
        jnp.transpose(kernels, (0, 1, 3, 2, 4)),
        jnp.asarray(weight_lanes(coils)),
        ky_start,
        kz_start,
        jnp.asarray(row_order(coils)),
        jnp.asarray(slab_order(2 * coils)),
        acquired_at,
        jnp.asarray(lane_order(cells, width)),
    ]
    held = [pltpu.SMEM(o.shape, o.dtype) if o.ndim == 1 else pltpu.VMEM(o.shape, o.dtype) for o in operands]
    filled = pl.pallas_call(
        functools.partial(kernel, nkz, ngx),
        out_shape=jax.ShapeDtypeStruct((2 * xs, 2 * coils, 3 * cells), jnp.bfloat16),
        in_specs=[pl.BlockSpec(memory_space=pltpu.HBM)] * len(operands),
        out_specs=pl.BlockSpec(memory_space=pltpu.VMEM),
        scratch_shapes=held + [
            lattice,
            lattice,
            pltpu.VMEM((16 * coils, taps), jnp.bfloat16),
            pltpu.VMEM((nkz, ngx, xs, 128), jnp.bfloat16),
            pltpu.VMEM((ngx, xs, 128), jnp.bfloat16),
            pltpu.VMEM((14 * coils, taps), jnp.bfloat16),
            pltpu.VMEM((xs // each * 4 * coils, 3 * 128), jnp.bfloat16),
            pltpu.SemaphoreType.DMA((len(operands),)),
            pltpu.SemaphoreType.DMA((ngx,)),
            pltpu.SemaphoreType.DMA((ngx,)),
            pltpu.SemaphoreType.DMA((nkz, ngx)),
            pltpu.SemaphoreType.DMA((nkz, ngx)),
        ],
        compiler_params=pltpu.CompilerParams(
            collective_id=0, has_side_effects=True, vmem_limit_bytes=LIMIT),
    )(*operands)
    return filled.reshape(2, xs, coils, 2, 3 * cells)


def solution(mesh):
    placed = (P(None, "kz", "gx", None, None), P("kz", None), P(), P(), P())
    return jax.shard_map(
        local,
        mesh=mesh,
        in_specs=placed,
        out_specs=P(None, "gx", None, "kz", None),
        check_vma=False,
    )
```

```python
import functools
import math

import jax
import jax.numpy as jnp
import ml_dtypes
import numpy as np
from jax import lax
from jax.experimental import pallas as pl
from jax.experimental.pallas import tpu as pltpu
from jax.sharding import PartitionSpec as P

BF16 = ml_dtypes.bfloat16
MESH = pl.DeviceIdType.MESH
GROUP = 4
EDGE = 4
LIMIT = 60 * 1024 * 1024


def readout_table(extent):
    index = np.arange(extent)
    angle = (index[:, None] * index[None, :] % extent) * (2.0 * math.pi / extent)
    return np.concatenate([np.cos(angle), np.sin(angle)], axis=1).astype(np.float64) / math.sqrt(extent)


def line_order(coils, cells):
    order = np.zeros((2, cells, 2, coils, coils, cells, 2), np.float32)
    for c in range(coils):
        for a in range(cells):
            order[0, a, 0, c, c, a, 0] = 1
            order[0, a, 1, c, c, a, 1] = 1
            order[1, a, 0, c, c, a, 1] = -1
            order[1, a, 1, c, c, a, 0] = 1
    return order.reshape(4 * cells * coils, 2 * coils * cells).astype(BF16)


def slab_order(values):
    order = np.zeros((GROUP, GROUP, values, GROUP, GROUP, values), np.float32)
    for b in range(GROUP):
        for a in range(GROUP):
            for v in range(values):
                order[b, a, v, a, b, v] = 1
    return order.reshape(GROUP * GROUP * values, -1).astype(BF16)


def weight_lanes(coils):
    lanes = np.zeros((2, 2, coils, 2, 2, GROUP, 2, coils), np.float32)
    for v in range(2):
        sign = -1 if v else 1
        for c in range(coils):
            lanes[0, v, c, 0, v, :, 0, c] = 1
            lanes[1, v, c, 0, v, :, 1, c] = -sign
            lanes[1, v, c, 1, v, :, 0, c] = 1
            lanes[0, v, c, 1, v, :, 1, c] = sign
    return lanes.reshape(2, 2 * coils, -1).astype(BF16)


def row_order(coils):
    values = 2 * coils
    order = np.zeros((4, values, 2, 7 * values), np.float32)
    for n in range(values):
        for rz in range(2):
            for ry in range(3):
                order[ry, n, rz, (ry * 2 + rz) * values + n] = 1
            order[3, n, rz, 6 * values + n] = 1
    return order.reshape(8 * values, 7 * values).astype(BF16)


def lane_order(cells, width):
    each = 128 // cells
    order = np.zeros((3, each, cells, each, width), np.float32)
    for ry in range(3):
        for x in range(each):
            for a in range(cells):
                order[ry, x, a, x, 3 * a + ry] = 1
    return order.reshape(3 * 128, each * width).astype(BF16)


def nt(left, right):
    return lax.dot_general(left, right, (((1,), (1,)), ((), ())), preferred_element_type=jnp.float32)


def kernel(nkz, ngx, *refs):
    sources, out, held = refs[:11], refs[11], refs[12:23]
    lines, order, table, parts, to_lanes, ky_start, kz_start, to_rows, to_slabs, acquired, to_ky = held
    near, far, weights, planes, spectra, natural, chosen, staged, load, unload, send_x, recv_x, send_z, recv_z = refs[23:]
    b, g = lax.axis_index("kz"), lax.axis_index("gx")
    barrier = pltpu.get_barrier_semaphore()
    for k in range(1, ngx):
        pl.semaphore_signal(barrier, inc=1, device_id=(b, lax.rem(g + k, ngx)), device_id_type=MESH)
    for j in range(1, nkz):
        pl.semaphore_signal(barrier, inc=1, device_id=(lax.rem(b + j, nkz), g), device_id_type=MESH)
    loading = [pltpu.make_async_copy(*pair, load.at[n]) for n, pair in enumerate(zip(sources, held))]
    for copy in loading:
        copy.start()

    f32, bf16 = jnp.float32, jnp.bfloat16
    sets = nkz // GROUP
    coils = parts.shape[3]
    values = 2 * coils
    cells = ngx * GROUP
    pitch = cells + 2 * EDGE
    xs = spectra.shape[1]

    count = values * GROUP
    for copy in loading[:2]:
        copy.wait()
    both = jnp.dot(order[...], lines[...].reshape(count, table.shape[0]), preferred_element_type=f32).astype(bf16)
    right = jnp.concatenate([both[:count], both[count:]], axis=1)
    loading[2].wait()
    spectra[...] = nt(table[...], right).astype(bf16).reshape(spectra.shape)
    planes[b, g] = spectra[g]

    pl.semaphore_wait(barrier, ngx + nkz - 2)
    along_x, along_z = {}, {}

    def forward(k):
        source = lax.rem(g + ngx - k, ngx)
        for j in range(1, nkz):
            along_z[j, k] = pltpu.make_async_remote_copy(
                src_ref=planes.at[b, source], dst_ref=planes.at[b, source], send_sem=send_z.at[j, k],
                recv_sem=recv_z.at[j, k], device_id=(lax.rem(b + j, nkz), g), device_id_type=MESH)
            along_z[j, k].start()

    for k in range(1, ngx):
        to = lax.rem(g + k, ngx)
        along_x[k] = pltpu.make_async_remote_copy(
            src_ref=spectra.at[to], dst_ref=planes.at[b, g], send_sem=send_x.at[k],
            recv_sem=recv_x.at[k], device_id=(b, to), device_id_type=MESH)
        along_x[k].start()
    forward(0)

    for copy in loading[3:]:
        copy.wait()
    terms = (
        jnp.dot(parts[0].reshape(36 * coils, values), to_lanes[0], preferred_element_type=f32)
        + jnp.dot(parts[1].reshape(36 * coils, values), to_lanes[1], preferred_element_type=f32)
    )

    lane = lax.broadcasted_iota(jnp.int32, (coils, 128), 1)
    slab = lane // values

    def place(t):
        here = {n: jnp.full((coils, 128), ky_start[t], jnp.int32) == n for n in (-2, -1, 0)}
        for v in range(2):
            for part in range(sets):
                cell = slab + part * GROUP
                if v:
                    cell = nkz - 1 - cell
                point = cell - b - kz_start[t]
                for s in range(2):
                    column = (s * 2 + v) * 128
                    rows = []
                    for i in range(3):
                        at = (t * 6 + i) * coils
                        first = terms[at : at + coils, column : column + 128]
                        second = terms[at + 3 * coils : at + 4 * coils, column : column + 128]
                        rows.append(jnp.where(point == 0, first, jnp.where(point == 1, second, 0.0)))
                    for d in range(-2, 3):
                        total = jnp.zeros((coils, 128), f32)
                        for i in range(3):
                            if -2 <= d - i <= 0:
                                total = jnp.where(here[d - i], rows[i], total)
                        where = ((v * 5 + d + 2) * sets + part) * 128
                        natural[(t * 2 + s) * coils : (t * 2 + s + 1) * coils, where : where + 128] = total.astype(bf16)

    def place_rest():
        natural[12 * coils :, :] = jnp.zeros((values, natural.shape[1]), bf16)
        row = lax.broadcasted_iota(jnp.int32, (values, 128), 0)
        wide = lax.broadcasted_iota(jnp.int32, (values, 128), 1)
        for part in range(sets):
            same = (b - part * GROUP) * values + row == wide
            where = (2 * sets + part) * 128
            natural[12 * coils :, where : where + 128] = jnp.where(same, 1.0, 0.0).astype(bf16)
        for x in range(sets * xs):
            for buffer in (near, far):
                buffer[x * pitch : x * pitch + EDGE, :] = jnp.zeros((EDGE, 128), f32)
                buffer[(x + 1) * pitch - EDGE : (x + 1) * pitch, :] = jnp.zeros((EDGE, 128), f32)

    work = [functools.partial(place, t) for t in range(6)] + [place_rest]
    for k in range(1, ngx):
        along_x[k].wait_recv()
        forward(k)
        if work:
            work.pop(0)()
    weights[...] = jnp.dot(to_rows[...], natural[...], preferred_element_type=f32).astype(bf16)

    for k in range(ngx):
        for j in range(1, nkz):
            along_z[j, k].wait_recv()
        source = lax.rem(g + ngx - k, ngx)
        for part in range(sets):
            block = jnp.concatenate([planes[part * GROUP + n, source] for n in range(GROUP)], axis=1)
            turned = jnp.dot(block, to_slabs[...], preferred_element_type=f32)
            for n in range(GROUP):
                piece = turned[:, n * 128 : (n + 1) * 128]
                base = part * xs * pitch + EDGE
                near[pl.ds(base + source * GROUP + n, xs, stride=pitch), :] = piece
                far[pl.ds(base + cells - 1 - n - source * GROUP, xs, stride=pitch), :] = piece

    each = 128 // cells
    width = to_ky.shape[1] // each
    step = 2 * each
    odd = lax.broadcasted_iota(jnp.int32, (2 * values, 2 * 128), 0) % 2
    position = jnp.concatenate([acquired[...]] * step, axis=1) - odd
    for start in range(0, xs, step):
        pieces = []
        for buffer in (near, far):
            for d in range(-2, 3):
                for part in range(sets):
                    rows = [(part * xs + x) * pitch + EDGE + d for x in range(start, start + step)]
                    pieces.append(jnp.concatenate([buffer[r : r + cells, :] for r in rows], axis=0).astype(bf16))
        result = nt(weights[...], jnp.concatenate(pieces, axis=1))
        actual = result[6 * values :]
        for ry in range(3):
            estimate = result[ry * 2 * values : (ry + 1) * 2 * values]
            picked = jnp.where(position == 2 * ry, actual, estimate).astype(bf16)
            for half in range(2):
                at = (start // each + half) * 2 * values
                chosen[at : at + 2 * values, ry * 128 : (ry + 1) * 128] = picked[:, half * 128 : (half + 1) * 128]
    batch = chosen.shape[0] // 2
    leaving = []
    for at in range(0, 2 * batch, batch):
        spread = jnp.dot(chosen[at : at + batch, :], to_ky[...], preferred_element_type=f32).astype(bf16)
        for row in range(0, batch, 2 * values):
            for n in range(each):
                x = (at + row) // (2 * values) * each + n
                for s in range(2):
                    first = row + s * values
                    staged[s * xs + x] = spread[first : first + values, n * width : n * width + 3 * cells]
        half = xs * batch // chosen.shape[0]
        for s in range(2):
            part = pl.ds(s * xs + at // batch * half, half)
            leaving.append(pltpu.make_async_copy(staged.at[part], out.at[part], unload.at[len(leaving)]))
            leaving[-1].start()
    for copy in list(along_x.values()) + list(along_z.values()):
        copy.wait_send()
    for copy in leaving:
        copy.wait()


def copy_kernel(source, target, sems):
    count = sems.shape[0]
    size = source.shape[0] // count
    copies = [
        pltpu.make_async_copy(source.at[pl.ds(n * size, size)], target.at[pl.ds(n * size, size)], sems.at[n])
        for n in range(count)
    ]
    for copy in copies:
        copy.start()
    for copy in copies:
        copy.wait()


def local(kspace_lines, acquired_at, ky_start, kz_start, kernels):
    nkz, ngx = lax.axis_size("kz"), lax.axis_size("gx")
    coils, _, own, _, extent = kspace_lines.shape
    xs, cells = extent // ngx, ngx * own
    assert own == GROUP and nkz % GROUP == 0 and 2 * coils * GROUP == 128 and 128 % cells == 0
    each = 128 // cells
    width = -(-3 * cells // 128) * 128
    sets = nkz // GROUP
    taps = 10 * 128 * sets
    lattice = pltpu.VMEM((sets * xs * (cells + 2 * EDGE), 128), jnp.float32)
    operands = [
        kspace_lines,
        jnp.asarray(line_order(coils, own)),
        jnp.asarray(readout_table(extent).astype(BF16)),
        jnp.transpose(kernels, (0, 1, 3, 2, 4)),
        jnp.asarray(weight_lanes(coils)),
        ky_start,
        kz_start,
        jnp.asarray(row_order(coils)),
        jnp.asarray(slab_order(2 * coils)),
        acquired_at,
        jnp.asarray(lane_order(cells, width)),
    ]
    held = [pltpu.SMEM(o.shape, o.dtype) if o.ndim == 1 else pltpu.VMEM(o.shape, o.dtype) for o in operands]
    filled = pl.pallas_call(
        functools.partial(kernel, nkz, ngx),
        out_shape=jax.ShapeDtypeStruct((2 * xs, 2 * coils, 3 * cells), jnp.bfloat16),
        in_specs=[pl.BlockSpec(memory_space=pltpu.HBM)] * len(operands),
        out_specs=pl.BlockSpec(memory_space=pltpu.HBM),
        scratch_shapes=held + [
            lattice,
            lattice,
            pltpu.VMEM((16 * coils, taps), jnp.bfloat16),
            pltpu.VMEM((nkz, ngx, xs, 128), jnp.bfloat16),
            pltpu.VMEM((ngx, xs, 128), jnp.bfloat16),
            pltpu.VMEM((14 * coils, taps), jnp.bfloat16),
            pltpu.VMEM((xs // each * 4 * coils, 3 * 128), jnp.bfloat16),
            pltpu.VMEM((2 * xs, 2 * coils, 3 * cells), jnp.bfloat16),
            pltpu.SemaphoreType.DMA((len(operands),)),
            pltpu.SemaphoreType.DMA((4,)),
            pltpu.SemaphoreType.DMA((ngx,)),
            pltpu.SemaphoreType.DMA((ngx,)),
            pltpu.SemaphoreType.DMA((nkz, ngx)),
            pltpu.SemaphoreType.DMA((nkz, ngx)),
        ],
        compiler_params=pltpu.CompilerParams(
            collective_id=0, has_side_effects=True, vmem_limit_bytes=LIMIT),
    )(*operands)
    filled = pl.pallas_call(
        copy_kernel,
        out_shape=jax.ShapeDtypeStruct(filled.shape, filled.dtype),
        in_specs=[pl.BlockSpec(memory_space=pltpu.HBM)],
        out_specs=pl.BlockSpec(memory_space=pltpu.HBM),
        scratch_shapes=[pltpu.SemaphoreType.DMA((8,))],
        compiler_params=pltpu.CompilerParams(vmem_limit_bytes=LIMIT),
    )(filled)
    return filled.reshape(2, xs, coils, 2, 3 * cells)


def solution(mesh):
    placed = (P(None, "kz", "gx", None, None), P("kz", None), P(), P(), P())
    return jax.shard_map(
        local,
        mesh=mesh,
        in_specs=placed,
        out_specs=P(None, "gx", None, "kz", None),
        check_vma=False,
    )
```

```python
import functools
import math

import jax
import jax.numpy as jnp
import ml_dtypes
import numpy as np
from jax import lax
from jax.experimental import pallas as pl
from jax.experimental.pallas import tpu as pltpu
from jax.sharding import PartitionSpec as P

BF16 = ml_dtypes.bfloat16
MESH = pl.DeviceIdType.MESH
GROUP = 4
EDGE = 4
LIMIT = 60 * 1024 * 1024


def readout_table(extent):
    index = np.arange(extent)
    angle = (index[:, None] * index[None, :] % extent) * (2.0 * math.pi / extent)
    return np.concatenate([np.cos(angle), np.sin(angle)], axis=1).astype(np.float64) / math.sqrt(extent)


def line_order(coils, cells):
    order = np.zeros((2, cells, 2, coils, coils, cells, 2), np.float32)
    for c in range(coils):
        for a in range(cells):
            order[0, a, 0, c, c, a, 0] = 1
            order[0, a, 1, c, c, a, 1] = 1
            order[1, a, 0, c, c, a, 1] = -1
            order[1, a, 1, c, c, a, 0] = 1
    return order.reshape(4 * cells * coils, 2 * coils * cells).astype(BF16)


def slab_order(values):
    order = np.zeros((GROUP, GROUP, values, GROUP, GROUP, values), np.float32)
    for b in range(GROUP):
        for a in range(GROUP):
            for v in range(values):
                order[b, a, v, a, b, v] = 1
    return order.reshape(GROUP * GROUP * values, -1).astype(BF16)


def weight_lanes(coils):
    lanes = np.zeros((2, 2, coils, 2, 2, GROUP, 2, coils), np.float32)
    for v in range(2):
        sign = -1 if v else 1
        for c in range(coils):
            lanes[0, v, c, 0, v, :, 0, c] = 1
            lanes[1, v, c, 0, v, :, 1, c] = -sign
            lanes[1, v, c, 1, v, :, 0, c] = 1
            lanes[0, v, c, 1, v, :, 1, c] = sign
    return lanes.reshape(2, 2 * coils, -1).astype(BF16)


def row_order(coils):
    values = 2 * coils
    order = np.zeros((4, values, 2, 7 * values), np.float32)
    for n in range(values):
        for rz in range(2):
            for ry in range(3):
                order[ry, n, rz, (ry * 2 + rz) * values + n] = 1
            order[3, n, rz, 6 * values + n] = 1
    return order.reshape(8 * values, 7 * values).astype(BF16)


def lane_order(cells, width):
    each = 128 // cells
    order = np.zeros((3, each, cells, each, width), np.float32)
    for ry in range(3):
        for x in range(each):
            for a in range(cells):
                order[ry, x, a, x, 3 * a + ry] = 1
    return order.reshape(3 * 128, each * width).astype(BF16)


def nt(left, right):
    return lax.dot_general(left, right, (((1,), (1,)), ((), ())), preferred_element_type=jnp.float32)


def kernel(nkz, ngx, *refs):
    sources, out, held = refs[:11], refs[11], refs[12:23]
    lines, order, table, parts, to_lanes, ky_start, kz_start, to_rows, to_slabs, acquired, to_ky = held
    near, far, weights, planes, spectra, natural, chosen, staged, load, unload, send_x, recv_x, send_z, recv_z = refs[23:]
    b, g = lax.axis_index("kz"), lax.axis_index("gx")
    barrier = pltpu.get_barrier_semaphore()
    for k in range(1, ngx):
        pl.semaphore_signal(barrier, inc=1, device_id=(b, lax.rem(g + k, ngx)), device_id_type=MESH)
    for j in range(1, nkz):
        pl.semaphore_signal(barrier, inc=1, device_id=(lax.rem(b + j, nkz), g), device_id_type=MESH)
    loading = [pltpu.make_async_copy(*pair, load.at[n]) for n, pair in enumerate(zip(sources, held))]
    for copy in loading:
        copy.start()

    f32, bf16 = jnp.float32, jnp.bfloat16
    sets = nkz // GROUP
    coils = parts.shape[3]
    values = 2 * coils
    cells = ngx * GROUP
    pitch = cells + 2 * EDGE
    xs = spectra.shape[1]

    count = values * GROUP
    for copy in loading[:2]:
        copy.wait()
    both = jnp.dot(order[...], lines[...].reshape(count, table.shape[0]), preferred_element_type=f32).astype(bf16)
    right = jnp.concatenate([both[:count], both[count:]], axis=1)
    loading[2].wait()
    spectra[...] = nt(table[...], right).astype(bf16).reshape(spectra.shape)
    planes[b, g] = spectra[g]

    pl.semaphore_wait(barrier, ngx + nkz - 2)
    along_x, along_z = {}, {}

    def forward(k):
        source = lax.rem(g + ngx - k, ngx)
        for j in range(1, nkz):
            along_z[j, k] = pltpu.make_async_remote_copy(
                src_ref=planes.at[b, source], dst_ref=planes.at[b, source], send_sem=send_z.at[j, k],
                recv_sem=recv_z.at[j, k], device_id=(lax.rem(b + j, nkz), g), device_id_type=MESH)
            along_z[j, k].start()

    for k in range(1, ngx):
        to = lax.rem(g + k, ngx)
        along_x[k] = pltpu.make_async_remote_copy(
            src_ref=spectra.at[to], dst_ref=planes.at[b, g], send_sem=send_x.at[k],
            recv_sem=recv_x.at[k], device_id=(b, to), device_id_type=MESH)
        along_x[k].start()
    forward(0)

    for copy in loading[3:]:
        copy.wait()
    terms = (
        jnp.dot(parts[0].reshape(36 * coils, values), to_lanes[0], preferred_element_type=f32)
        + jnp.dot(parts[1].reshape(36 * coils, values), to_lanes[1], preferred_element_type=f32)
    )

    lane = lax.broadcasted_iota(jnp.int32, (coils, 128), 1)
    slab = lane // values

    def place(t):
        here = {n: jnp.full((coils, 128), ky_start[t], jnp.int32) == n for n in (-2, -1, 0)}
        for v in range(2):
            for part in range(sets):
                cell = slab + part * GROUP
                if v:
                    cell = nkz - 1 - cell
                point = cell - b - kz_start[t]
                for s in range(2):
                    column = (s * 2 + v) * 128
                    rows = []
                    for i in range(3):
                        at = (t * 6 + i) * coils
                        first = terms[at : at + coils, column : column + 128]
                        second = terms[at + 3 * coils : at + 4 * coils, column : column + 128]
                        rows.append(jnp.where(point == 0, first, jnp.where(point == 1, second, 0.0)))
                    for d in range(-2, 3):
                        total = jnp.zeros((coils, 128), f32)
                        for i in range(3):
                            if -2 <= d - i <= 0:
                                total = jnp.where(here[d - i], rows[i], total)
                        where = ((v * 5 + d + 2) * sets + part) * 128
                        natural[(t * 2 + s) * coils : (t * 2 + s + 1) * coils, where : where + 128] = total.astype(bf16)

    def place_rest():
        natural[12 * coils :, :] = jnp.zeros((values, natural.shape[1]), bf16)
        row = lax.broadcasted_iota(jnp.int32, (values, 128), 0)
        wide = lax.broadcasted_iota(jnp.int32, (values, 128), 1)
        for part in range(sets):
            same = (b - part * GROUP) * values + row == wide
            where = (2 * sets + part) * 128
            natural[12 * coils :, where : where + 128] = jnp.where(same, 1.0, 0.0).astype(bf16)
        for x in range(sets * xs):
            for buffer in (near, far):
                buffer[x * pitch : x * pitch + EDGE, :] = jnp.zeros((EDGE, 128), f32)
                buffer[(x + 1) * pitch - EDGE : (x + 1) * pitch, :] = jnp.zeros((EDGE, 128), f32)

    work = [functools.partial(place, t) for t in range(6)] + [place_rest]
    for k in range(1, ngx):
        along_x[k].wait_recv()
        forward(k)
        if work:
            work.pop(0)()
    weights[...] = jnp.dot(to_rows[...], natural[...], preferred_element_type=f32).astype(bf16)

    for k in range(ngx):
        for j in range(1, nkz):
            along_z[j, k].wait_recv()
        source = lax.rem(g + ngx - k, ngx)
        for part in range(sets):
            block = jnp.concatenate([planes[part * GROUP + n, source] for n in range(GROUP)], axis=1)
            turned = jnp.dot(block, to_slabs[...], preferred_element_type=f32)
            for n in range(GROUP):
                piece = turned[:, n * 128 : (n + 1) * 128]
                base = part * xs * pitch + EDGE
                near[pl.ds(base + source * GROUP + n, xs, stride=pitch), :] = piece
                far[pl.ds(base + cells - 1 - n - source * GROUP, xs, stride=pitch), :] = piece

    each = 128 // cells
    width = to_ky.shape[1] // each
    step = 2 * each
    odd = lax.broadcasted_iota(jnp.int32, (2 * values, 2 * 128), 0) % 2
    position = jnp.concatenate([acquired[...]] * step, axis=1) - odd
    for start in range(0, xs, step):
        pieces = []
        for buffer in (near, far):
            for d in range(-2, 3):
                for part in range(sets):
                    rows = [(part * xs + x) * pitch + EDGE + d for x in range(start, start + step)]
                    pieces.append(jnp.concatenate([buffer[r : r + cells, :] for r in rows], axis=0).astype(bf16))
        result = nt(weights[...], jnp.concatenate(pieces, axis=1))
        actual = result[6 * values :]
        for ry in range(3):
            estimate = result[ry * 2 * values : (ry + 1) * 2 * values]
            picked = jnp.where(position == 2 * ry, actual, estimate).astype(bf16)
            for half in range(2):
                at = (start // each + half) * 2 * values
                chosen[at : at + 2 * values, ry * 128 : (ry + 1) * 128] = picked[:, half * 128 : (half + 1) * 128]
    batch = chosen.shape[0] // 2
    leaving = []
    for at in range(0, 2 * batch, batch):
        spread = jnp.dot(chosen[at : at + batch, :], to_ky[...], preferred_element_type=f32).astype(bf16)
        for row in range(0, batch, 2 * values):
            for n in range(each):
                x = (at + row) // (2 * values) * each + n
                for s in range(2):
                    first = row + s * values
                    staged[s * xs + x] = spread[first : first + values, n * width : n * width + 3 * cells]
        half = xs * batch // chosen.shape[0]
        for s in range(2):
            part = pl.ds(s * xs + at // batch * half, half)
            leaving.append(pltpu.make_async_copy(staged.at[part], out.at[part], unload.at[len(leaving)]))
            leaving[-1].start()
    for copy in list(along_x.values()) + list(along_z.values()):
        copy.wait_send()
    for copy in leaving:
        copy.wait()


def copy_kernel(source, target, held, entering, leaving):
    count = entering.shape[0]
    size = source.shape[0] // count
    pairs = []
    for n in range(count):
        part = pl.ds(n * size, size)
        pairs.append((
            pltpu.make_async_copy(source.at[part], held.at[part], entering.at[n]),
            pltpu.make_async_copy(held.at[part], target.at[part], leaving.at[n]),
        ))
    for first, _ in pairs:
        first.start()
    for first, second in pairs:
        first.wait()
        second.start()
    for _, second in pairs:
        second.wait()


def local(kspace_lines, acquired_at, ky_start, kz_start, kernels):
    nkz, ngx = lax.axis_size("kz"), lax.axis_size("gx")
    coils, _, own, _, extent = kspace_lines.shape
    xs, cells = extent // ngx, ngx * own
    assert own == GROUP and nkz % GROUP == 0 and 2 * coils * GROUP == 128 and 128 % cells == 0
    each = 128 // cells
    width = -(-3 * cells // 128) * 128
    sets = nkz // GROUP
    taps = 10 * 128 * sets
    lattice = pltpu.VMEM((sets * xs * (cells + 2 * EDGE), 128), jnp.float32)
    operands = [
        kspace_lines,
        jnp.asarray(line_order(coils, own)),
        jnp.asarray(readout_table(extent).astype(BF16)),
        jnp.transpose(kernels, (0, 1, 3, 2, 4)),
        jnp.asarray(weight_lanes(coils)),
        ky_start,
        kz_start,
        jnp.asarray(row_order(coils)),
        jnp.asarray(slab_order(2 * coils)),
        acquired_at,
        jnp.asarray(lane_order(cells, width)),
    ]
    held = [pltpu.SMEM(o.shape, o.dtype) if o.ndim == 1 else pltpu.VMEM(o.shape, o.dtype) for o in operands]
    filled = pl.pallas_call(
        functools.partial(kernel, nkz, ngx),
        out_shape=jax.ShapeDtypeStruct((2 * xs, 2 * coils, 3 * cells), jnp.bfloat16),
        in_specs=[pl.BlockSpec(memory_space=pltpu.HBM)] * len(operands),
        out_specs=pl.BlockSpec(memory_space=pltpu.HBM),
        scratch_shapes=held + [
            lattice,
            lattice,
            pltpu.VMEM((16 * coils, taps), jnp.bfloat16),
            pltpu.VMEM((nkz, ngx, xs, 128), jnp.bfloat16),
            pltpu.VMEM((ngx, xs, 128), jnp.bfloat16),
            pltpu.VMEM((14 * coils, taps), jnp.bfloat16),
            pltpu.VMEM((xs // each * 4 * coils, 3 * 128), jnp.bfloat16),
            pltpu.VMEM((2 * xs, 2 * coils, 3 * cells), jnp.bfloat16),
            pltpu.SemaphoreType.DMA((len(operands),)),
            pltpu.SemaphoreType.DMA((4,)),
            pltpu.SemaphoreType.DMA((ngx,)),
            pltpu.SemaphoreType.DMA((ngx,)),
            pltpu.SemaphoreType.DMA((nkz, ngx)),
            pltpu.SemaphoreType.DMA((nkz, ngx)),
        ],
        compiler_params=pltpu.CompilerParams(
            collective_id=0, has_side_effects=True, vmem_limit_bytes=LIMIT),
    )(*operands)
    filled = pl.pallas_call(
        copy_kernel,
        out_shape=jax.ShapeDtypeStruct(filled.shape, filled.dtype),
        in_specs=[pl.BlockSpec(memory_space=pltpu.HBM)],
        out_specs=pl.BlockSpec(memory_space=pltpu.HBM),
        scratch_shapes=[
            pltpu.VMEM(filled.shape, filled.dtype),
            pltpu.SemaphoreType.DMA((8,)),
            pltpu.SemaphoreType.DMA((8,)),
        ],
        compiler_params=pltpu.CompilerParams(vmem_limit_bytes=LIMIT),
    )(filled)
    return filled.reshape(2, xs, coils, 2, 3 * cells)


def solution(mesh):
    placed = (P(None, "kz", "gx", None, None), P("kz", None), P(), P(), P())
    return jax.shard_map(
        local,
        mesh=mesh,
        in_specs=placed,
        out_specs=P(None, "gx", None, "kz", None),
        check_vma=False,
    )
```

```python
import functools
import math

import jax
import jax.numpy as jnp
import ml_dtypes
import numpy as np
from jax import lax
from jax.experimental import pallas as pl
from jax.experimental.pallas import tpu as pltpu
from jax.sharding import PartitionSpec as P

BF16 = ml_dtypes.bfloat16
MESH = pl.DeviceIdType.MESH
GROUP = 4
EDGE = 4
LIMIT = 60 * 1024 * 1024


def readout_table(extent):
    index = np.arange(extent)
    angle = (index[:, None] * index[None, :] % extent) * (2.0 * math.pi / extent)
    return np.concatenate([np.cos(angle), np.sin(angle)], axis=1).astype(np.float64) / math.sqrt(extent)


def line_order(coils, cells):
    order = np.zeros((2, cells, 2, coils, coils, cells, 2), np.float32)
    for c in range(coils):
        for a in range(cells):
            order[0, a, 0, c, c, a, 0] = 1
            order[0, a, 1, c, c, a, 1] = 1
            order[1, a, 0, c, c, a, 1] = -1
            order[1, a, 1, c, c, a, 0] = 1
    return order.reshape(4 * cells * coils, 2 * coils * cells).astype(BF16)


def slab_order(values):
    order = np.zeros((GROUP, GROUP, values, GROUP, GROUP, values), np.float32)
    for b in range(GROUP):
        for a in range(GROUP):
            for v in range(values):
                order[b, a, v, a, b, v] = 1
    return order.reshape(GROUP * GROUP * values, -1).astype(BF16)


def weight_lanes(coils):
    lanes = np.zeros((2, 2, coils, 2, 2, GROUP, 2, coils), np.float32)
    for v in range(2):
        sign = -1 if v else 1
        for c in range(coils):
            lanes[0, v, c, 0, v, :, 0, c] = 1
            lanes[1, v, c, 0, v, :, 1, c] = -sign
            lanes[1, v, c, 1, v, :, 0, c] = 1
            lanes[0, v, c, 1, v, :, 1, c] = sign
    return lanes.reshape(2, 2 * coils, -1).astype(BF16)


def row_order(coils):
    values = 2 * coils
    order = np.zeros((4, values, 2, 7 * values), np.float32)
    for n in range(values):
        for rz in range(2):
            for ry in range(3):
                order[ry, n, rz, (ry * 2 + rz) * values + n] = 1
            order[3, n, rz, 6 * values + n] = 1
    return order.reshape(8 * values, 7 * values).astype(BF16)


def lane_order(cells, width):
    each = 128 // cells
    order = np.zeros((3, each, cells, each, width), np.float32)
    for ry in range(3):
        for x in range(each):
            for a in range(cells):
                order[ry, x, a, x, 3 * a + ry] = 1
    return order.reshape(3 * 128, each * width).astype(BF16)


def nt(left, right):
    return lax.dot_general(left, right, (((1,), (1,)), ((), ())), preferred_element_type=jnp.float32)


def kernel(nkz, ngx, *refs):
    sources, out, held = refs[:11], refs[11], refs[12:23]
    lines, order, table, parts, to_lanes, ky_start, kz_start, to_rows, to_slabs, acquired, to_ky = held
    near, far, weights, planes, spectra, natural, chosen, staged, load, unload, send_x, recv_x, send_z, recv_z = refs[23:]
    b, g = lax.axis_index("kz"), lax.axis_index("gx")
    barrier = pltpu.get_barrier_semaphore()
    for k in range(1, ngx):
        pl.semaphore_signal(barrier, inc=1, device_id=(b, lax.rem(g + k, ngx)), device_id_type=MESH)
    for j in range(1, nkz):
        pl.semaphore_signal(barrier, inc=1, device_id=(lax.rem(b + j, nkz), g), device_id_type=MESH)
    loading = [pltpu.make_async_copy(*pair, load.at[n]) for n, pair in enumerate(zip(sources, held))]
    for copy in loading:
        copy.start()

    f32, bf16 = jnp.float32, jnp.bfloat16
    sets = nkz // GROUP
    coils = parts.shape[3]
    values = 2 * coils
    cells = ngx * GROUP
    pitch = cells + 2 * EDGE
    _, halves, hx, _ = spectra.shape
    xs = halves * hx
    pairs = ngx // 2
    chip, core = g // 2, lax.rem(g, 2)

    count = values * GROUP
    for copy in loading[:2]:
        copy.wait()
    both = jnp.dot(order[...], lines[...].reshape(count, table.shape[0]), preferred_element_type=f32).astype(bf16)
    right = jnp.concatenate([both[:count], both[count:]], axis=1)
    loading[2].wait()
    spectra[...] = nt(table[...], right).astype(bf16).reshape(spectra.shape)
    for h in range(halves):
        planes[b, h, g] = spectra[g, h]

    pl.semaphore_wait(barrier, ngx + nkz - 2)
    along_x, along_z = {}, {}

    def forward(h, m):
        block = planes.at[b, h, pl.ds(2 * lax.rem(chip + pairs - m, pairs), 2)]
        for j in range(1, nkz):
            along_z[j, h, m] = pltpu.make_async_remote_copy(
                src_ref=block, dst_ref=block, send_sem=send_z.at[j, h, m], recv_sem=recv_z.at[j, h, m],
                device_id=(lax.rem(b + j, nkz), g), device_id_type=MESH)
            along_z[j, h, m].start()

    for h in range(halves):
        for k in range(1, ngx):
            to = 2 * lax.rem(chip + k // 2, pairs) + lax.rem(core + k % 2, 2)
            along_x[h, k] = pltpu.make_async_remote_copy(
                src_ref=spectra.at[to, h], dst_ref=planes.at[b, h, g], send_sem=send_x.at[h, k],
                recv_sem=recv_x.at[h, k], device_id=(b, to), device_id_type=MESH)
            along_x[h, k].start()
    along_x[0, 1].wait_recv()
    forward(0, 0)
    for copy in loading[3:]:
        copy.wait()
    terms = (
        jnp.dot(parts[0].reshape(36 * coils, values), to_lanes[0], preferred_element_type=f32)
        + jnp.dot(parts[1].reshape(36 * coils, values), to_lanes[1], preferred_element_type=f32)
    )

    lane = lax.broadcasted_iota(jnp.int32, (coils, 128), 1)
    slab = lane // values

    def place(t):
        here = {n: jnp.full((coils, 128), ky_start[t], jnp.int32) == n for n in (-2, -1, 0)}
        for v in range(2):
            for part in range(sets):
                cell = slab + part * GROUP
                if v:
                    cell = nkz - 1 - cell
                point = cell - b - kz_start[t]
                for s in range(2):
                    column = (s * 2 + v) * 128
                    rows = []
                    for i in range(3):
                        at = (t * 6 + i) * coils
                        first = terms[at : at + coils, column : column + 128]
                        second = terms[at + 3 * coils : at + 4 * coils, column : column + 128]
                        rows.append(jnp.where(point == 0, first, jnp.where(point == 1, second, 0.0)))
                    for d in range(-2, 3):
                        total = jnp.zeros((coils, 128), f32)
                        for i in range(3):
                            if -2 <= d - i <= 0:
                                total = jnp.where(here[d - i], rows[i], total)
                        where = ((v * 5 + d + 2) * sets + part) * 128
                        natural[(t * 2 + s) * coils : (t * 2 + s + 1) * coils, where : where + 128] = total.astype(bf16)

    def place_rest():
        natural[12 * coils :, :] = jnp.zeros((values, natural.shape[1]), bf16)
        row = lax.broadcasted_iota(jnp.int32, (values, 128), 0)
        wide = lax.broadcasted_iota(jnp.int32, (values, 128), 1)
        for part in range(sets):
            same = (b - part * GROUP) * values + row == wide
            where = (2 * sets + part) * 128
            natural[12 * coils :, where : where + 128] = jnp.where(same, 1.0, 0.0).astype(bf16)
        for x in range(sets * xs):
            for buffer in (near, far):
                buffer[x * pitch : x * pitch + EDGE, :] = jnp.zeros((EDGE, 128), f32)
                buffer[(x + 1) * pitch - EDGE : (x + 1) * pitch, :] = jnp.zeros((EDGE, 128), f32)

    work = [functools.partial(place, t) for t in range(6)] + [place_rest]
    for h in range(halves):
        for m in range(pairs):
            if h or m:
                for k in range(max(2 * m, 1), 2 * m + 2):
                    along_x[h, k].wait_recv()
                forward(h, m)
            if work:
                work.pop(0)()
    for piece in work:
        piece()
    weights[...] = jnp.dot(to_rows[...], natural[...], preferred_element_type=f32).astype(bf16)

    def regroup(h):
        for m in range(pairs):
            for j in range(1, nkz):
                along_z[j, h, m].wait_recv()
        for part in range(sets):
            block = jnp.concatenate(
                [planes[part * GROUP + n, h].reshape(ngx * hx, 128) for n in range(GROUP)], axis=1)
            turned = jnp.dot(block, to_slabs[...], preferred_element_type=f32)
            base = (part * xs + h * hx) * pitch + EDGE
            for a in range(cells):
                q, n = a // GROUP, a % GROUP
                piece = turned[q * hx : (q + 1) * hx, n * 128 : (n + 1) * 128]
                near[pl.ds(base + a, hx, stride=pitch), :] = piece
                far[pl.ds(base + cells - 1 - a, hx, stride=pitch), :] = piece

    each = 128 // cells
    width = to_ky.shape[1] // each
    step = 2 * each
    odd = lax.broadcasted_iota(jnp.int32, (2 * values, 2 * 128), 0) % 2
    position = jnp.concatenate([acquired[...]] * step, axis=1) - odd
    batch = chosen.shape[0] // halves
    leaving = []
    for h in range(halves):
        regroup(h)
        for start in range(h * hx, (h + 1) * hx, step):
            pieces = []
            for buffer in (near, far):
                for d in range(-2, 3):
                    for part in range(sets):
                        rows = [(part * xs + x) * pitch + EDGE + d for x in range(start, start + step)]
                        pieces.append(jnp.concatenate([buffer[r : r + cells, :] for r in rows], axis=0).astype(bf16))
            result = nt(weights[...], jnp.concatenate(pieces, axis=1))
            actual = result[6 * values :]
            for ry in range(3):
                estimate = result[ry * 2 * values : (ry + 1) * 2 * values]
                picked = jnp.where(position == 2 * ry, actual, estimate).astype(bf16)
                for half in range(2):
                    at = (start // each + half) * 2 * values
                    chosen[at : at + 2 * values, ry * 128 : (ry + 1) * 128] = picked[:, half * 128 : (half + 1) * 128]
        at = h * batch
        spread = jnp.dot(chosen[at : at + batch, :], to_ky[...], preferred_element_type=f32).astype(bf16)
        for row in range(0, batch, 2 * values):
            for n in range(each):
                x = (at + row) // (2 * values) * each + n
                for s in range(2):
                    first = row + s * values
                    staged[s * xs + x] = spread[first : first + values, n * width : n * width + 3 * cells]
        for s in range(2):
            part = pl.ds(s * xs + h * hx, hx)
            leaving.append(pltpu.make_async_copy(staged.at[part], out.at[part], unload.at[len(leaving)]))
            leaving[-1].start()
    for copy in list(along_x.values()) + list(along_z.values()):
        copy.wait_send()
    for copy in leaving:
        copy.wait()


def copy_kernel(source, target, held, entering, leaving):
    count = entering.shape[0]
    size = source.shape[0] // count
    pairs = []
    for n in range(count):
        part = pl.ds(n * size, size)
        pairs.append((
            pltpu.make_async_copy(source.at[part], held.at[part], entering.at[n]),
            pltpu.make_async_copy(held.at[part], target.at[part], leaving.at[n]),
        ))
    for first, _ in pairs:
        first.start()
    for first, second in pairs:
        first.wait()
        second.start()
    for _, second in pairs:
        second.wait()


def local(kspace_lines, acquired_at, ky_start, kz_start, kernels):
    nkz, ngx = lax.axis_size("kz"), lax.axis_size("gx")
    coils, _, own, _, extent = kspace_lines.shape
    xs, cells = extent // ngx, ngx * own
    assert own == GROUP and ngx % 2 == 0 and nkz % GROUP == 0 and 2 * coils * GROUP == 128 and 128 % cells == 0
    each = 128 // cells
    width = -(-3 * cells // 128) * 128
    sets = nkz // GROUP
    halves = 2 if xs % 32 == 0 else 1
    hx = xs // halves
    taps = 10 * 128 * sets
    lattice = pltpu.VMEM((sets * xs * (cells + 2 * EDGE), 128), jnp.float32)
    operands = [
        kspace_lines,
        jnp.asarray(line_order(coils, own)),
        jnp.asarray(readout_table(extent).astype(BF16)),
        jnp.transpose(kernels, (0, 1, 3, 2, 4)),
        jnp.asarray(weight_lanes(coils)),
        ky_start,
        kz_start,
        jnp.asarray(row_order(coils)),
        jnp.asarray(slab_order(2 * coils)),
        acquired_at,
        jnp.asarray(lane_order(cells, width)),
    ]
    held = [pltpu.SMEM(o.shape, o.dtype) if o.ndim == 1 else pltpu.VMEM(o.shape, o.dtype) for o in operands]
    filled = pl.pallas_call(
        functools.partial(kernel, nkz, ngx),
        out_shape=jax.ShapeDtypeStruct((2 * xs, 2 * coils, 3 * cells), jnp.bfloat16),
        in_specs=[pl.BlockSpec(memory_space=pltpu.HBM)] * len(operands),
        out_specs=pl.BlockSpec(memory_space=pltpu.HBM),
        scratch_shapes=held + [
            lattice,
            lattice,
            pltpu.VMEM((16 * coils, taps), jnp.bfloat16),
            pltpu.VMEM((nkz, halves, ngx, hx, 128), jnp.bfloat16),
            pltpu.VMEM((ngx, halves, hx, 128), jnp.bfloat16),
            pltpu.VMEM((14 * coils, taps), jnp.bfloat16),
            pltpu.VMEM((xs // each * 4 * coils, 3 * 128), jnp.bfloat16),
            pltpu.VMEM((2 * xs, 2 * coils, 3 * cells), jnp.bfloat16),
            pltpu.SemaphoreType.DMA((len(operands),)),
            pltpu.SemaphoreType.DMA((2 * halves,)),
            pltpu.SemaphoreType.DMA((halves, ngx)),
            pltpu.SemaphoreType.DMA((halves, ngx)),
            pltpu.SemaphoreType.DMA((nkz, halves, ngx // 2)),
            pltpu.SemaphoreType.DMA((nkz, halves, ngx // 2)),
        ],
        compiler_params=pltpu.CompilerParams(
            collective_id=0, has_side_effects=True, vmem_limit_bytes=LIMIT),
    )(*operands)
    filled = pl.pallas_call(
        copy_kernel,
        out_shape=jax.ShapeDtypeStruct(filled.shape, filled.dtype),
        in_specs=[pl.BlockSpec(memory_space=pltpu.HBM)],
        out_specs=pl.BlockSpec(memory_space=pltpu.HBM),
        scratch_shapes=[
            pltpu.VMEM(filled.shape, filled.dtype),
            pltpu.SemaphoreType.DMA((8,)),
            pltpu.SemaphoreType.DMA((8,)),
        ],
        compiler_params=pltpu.CompilerParams(vmem_limit_bytes=LIMIT),
    )(filled)
    return filled.reshape(2, xs, coils, 2, 3 * cells)


def solution(mesh):
    placed = (P(None, "kz", "gx", None, None), P("kz", None), P(), P(), P())
    return jax.shard_map(
        local,
        mesh=mesh,
        in_specs=placed,
        out_specs=P(None, "gx", None, "kz", None),
        check_vma=False,
    )
```

```python
import functools
import math

import jax
import jax.numpy as jnp
import ml_dtypes
import numpy as np
from jax import lax
from jax.experimental import pallas as pl
from jax.experimental.pallas import tpu as pltpu
from jax.sharding import PartitionSpec as P

BF16 = ml_dtypes.bfloat16
MESH = pl.DeviceIdType.MESH
GROUP = 4
EDGE = 4
PARTS = 4
LIMIT = 60 * 1024 * 1024


def readout_table(extent):
    index = np.arange(extent)
    angle = (index[:, None] * index[None, :] % extent) * (2.0 * math.pi / extent)
    return np.concatenate([np.cos(angle), np.sin(angle)], axis=1).astype(np.float64) / math.sqrt(extent)


def line_order(coils, cells):
    order = np.zeros((2, cells, 2, coils, coils, cells, 2), np.float32)
    for c in range(coils):
        for a in range(cells):
            order[0, a, 0, c, c, a, 0] = 1
            order[0, a, 1, c, c, a, 1] = 1
            order[1, a, 0, c, c, a, 1] = -1
            order[1, a, 1, c, c, a, 0] = 1
    return order.reshape(4 * cells * coils, 2 * coils * cells).astype(BF16)


def slab_order(values):
    order = np.zeros((GROUP, GROUP, values, GROUP, GROUP, values), np.float32)
    for b in range(GROUP):
        for a in range(GROUP):
            for v in range(values):
                order[b, a, v, a, b, v] = 1
    return order.reshape(GROUP * GROUP * values, -1).astype(BF16)


def weight_lanes(coils):
    lanes = np.zeros((2, 2, coils, 2, 2, GROUP, 2, coils), np.float32)
    for v in range(2):
        sign = -1 if v else 1
        for c in range(coils):
            lanes[0, v, c, 0, v, :, 0, c] = 1
            lanes[1, v, c, 0, v, :, 1, c] = -sign
            lanes[1, v, c, 1, v, :, 0, c] = 1
            lanes[0, v, c, 1, v, :, 1, c] = sign
    return lanes.reshape(2, 2 * coils, -1).astype(BF16)


def row_order(coils):
    values = 2 * coils
    order = np.zeros((4, values, 2, 7 * values), np.float32)
    for n in range(values):
        for rz in range(2):
            for ry in range(3):
                order[ry, n, rz, (ry * 2 + rz) * values + n] = 1
            order[3, n, rz, 6 * values + n] = 1
    return order.reshape(8 * values, 7 * values).astype(BF16)


def lane_order(cells, width):
    each = 128 // cells
    order = np.zeros((3, each, cells, each, width), np.float32)
    for ry in range(3):
        for x in range(each):
            for a in range(cells):
                order[ry, x, a, x, 3 * a + ry] = 1
    return order.reshape(3 * 128, each * width).astype(BF16)


def nt(left, right):
    return lax.dot_general(left, right, (((1,), (1,)), ((), ())), preferred_element_type=jnp.float32)


def kernel(nkz, ngx, *refs):
    sources, out, held = refs[:10], refs[10], refs[11:21]
    lines, order, table, parts, to_lanes, ky_start, kz_start, to_rows, to_slabs, acquired = held
    near, far, weights, planes, spectra, natural, chosen, load, unload, send_x, recv_x, send_z, recv_z = refs[21:]
    b, g = lax.axis_index("kz"), lax.axis_index("gx")
    barrier = pltpu.get_barrier_semaphore()
    for k in range(1, ngx):
        pl.semaphore_signal(barrier, inc=1, device_id=(b, lax.rem(g + k, ngx)), device_id_type=MESH)
    for j in range(1, nkz):
        pl.semaphore_signal(barrier, inc=1, device_id=(lax.rem(b + j, nkz), g), device_id_type=MESH)
    loading = [pltpu.make_async_copy(*pair, load.at[n]) for n, pair in enumerate(zip(sources, held))]
    for copy in loading:
        copy.start()

    f32, bf16 = jnp.float32, jnp.bfloat16
    sets = nkz // GROUP
    coils = parts.shape[3]
    values = 2 * coils
    cells = ngx * GROUP
    pitch = cells + 2 * EDGE
    _, halves, hx, _ = spectra.shape
    xs = halves * hx
    pairs = ngx // 2
    chip, core = g // 2, lax.rem(g, 2)

    count = values * GROUP
    for copy in loading[:2]:
        copy.wait()
    both = jnp.dot(order[...], lines[...].reshape(count, table.shape[0]), preferred_element_type=f32).astype(bf16)
    right = jnp.concatenate([both[:count], both[count:]], axis=1)
    loading[2].wait()
    spectra[...] = nt(table[...], right).astype(bf16).reshape(spectra.shape)
    for h in range(halves):
        planes[b, h, g] = spectra[g, h]

    pl.semaphore_wait(barrier, ngx + nkz - 2)
    along_x, along_z = {}, {}

    def forward(h, m):
        block = planes.at[b, h, pl.ds(2 * lax.rem(chip + pairs - m, pairs), 2)]
        for j in range(1, nkz):
            along_z[j, h, m] = pltpu.make_async_remote_copy(
                src_ref=block, dst_ref=block, send_sem=send_z.at[j, h, m], recv_sem=recv_z.at[j, h, m],
                device_id=(lax.rem(b + j, nkz), g), device_id_type=MESH)
            along_z[j, h, m].start()

    for h in range(halves):
        for k in range(1, ngx):
            to = 2 * lax.rem(chip + k // 2, pairs) + lax.rem(core + k % 2, 2)
            along_x[h, k] = pltpu.make_async_remote_copy(
                src_ref=spectra.at[to, h], dst_ref=planes.at[b, h, g], send_sem=send_x.at[h, k],
                recv_sem=recv_x.at[h, k], device_id=(b, to), device_id_type=MESH)
            along_x[h, k].start()
    along_x[0, 1].wait_recv()
    forward(0, 0)
    for copy in loading[3:]:
        copy.wait()
    terms = (
        jnp.dot(parts[0].reshape(36 * coils, values), to_lanes[0], preferred_element_type=f32)
        + jnp.dot(parts[1].reshape(36 * coils, values), to_lanes[1], preferred_element_type=f32)
    )

    lane = lax.broadcasted_iota(jnp.int32, (coils, 128), 1)
    slab = lane // values

    def place(t):
        here = {n: jnp.full((coils, 128), ky_start[t], jnp.int32) == n for n in (-2, -1, 0)}
        for v in range(2):
            for part in range(sets):
                cell = slab + part * GROUP
                if v:
                    cell = nkz - 1 - cell
                point = cell - b - kz_start[t]
                for s in range(2):
                    column = (s * 2 + v) * 128
                    rows = []
                    for i in range(3):
                        at = (t * 6 + i) * coils
                        first = terms[at : at + coils, column : column + 128]
                        second = terms[at + 3 * coils : at + 4 * coils, column : column + 128]
                        rows.append(jnp.where(point == 0, first, jnp.where(point == 1, second, 0.0)))
                    for d in range(-2, 3):
                        total = jnp.zeros((coils, 128), f32)
                        for i in range(3):
                            if -2 <= d - i <= 0:
                                total = jnp.where(here[d - i], rows[i], total)
                        where = ((v * 5 + d + 2) * sets + part) * 128
                        natural[(t * 2 + s) * coils : (t * 2 + s + 1) * coils, where : where + 128] = total.astype(bf16)

    def place_rest():
        natural[12 * coils :, :] = jnp.zeros((values, natural.shape[1]), bf16)
        row = lax.broadcasted_iota(jnp.int32, (values, 128), 0)
        wide = lax.broadcasted_iota(jnp.int32, (values, 128), 1)
        for part in range(sets):
            same = (b - part * GROUP) * values + row == wide
            where = (2 * sets + part) * 128
            natural[12 * coils :, where : where + 128] = jnp.where(same, 1.0, 0.0).astype(bf16)
        for x in range(sets * xs):
            for buffer in (near, far):
                buffer[x * pitch : x * pitch + EDGE, :] = jnp.zeros((EDGE, 128), f32)
                buffer[(x + 1) * pitch - EDGE : (x + 1) * pitch, :] = jnp.zeros((EDGE, 128), f32)

    work = [functools.partial(place, t) for t in range(6)] + [place_rest]
    for h in range(halves):
        for m in range(pairs):
            if h or m:
                for k in range(max(2 * m, 1), 2 * m + 2):
                    along_x[h, k].wait_recv()
                forward(h, m)
            if work:
                work.pop(0)()
    for piece in work:
        piece()
    weights[...] = jnp.dot(to_rows[...], natural[...], preferred_element_type=f32).astype(bf16)

    def regroup(h):
        for m in range(pairs):
            for j in range(1, nkz):
                along_z[j, h, m].wait_recv()
        for part in range(sets):
            block = jnp.concatenate(
                [planes[part * GROUP + n, h].reshape(ngx * hx, 128) for n in range(GROUP)], axis=1)
            turned = jnp.dot(block, to_slabs[...], preferred_element_type=f32)
            base = (part * xs + h * hx) * pitch + EDGE
            for a in range(cells):
                q, n = a // GROUP, a % GROUP
                piece = turned[q * hx : (q + 1) * hx, n * 128 : (n + 1) * 128]
                near[pl.ds(base + a, hx, stride=pitch), :] = piece
                far[pl.ds(base + cells - 1 - a, hx, stride=pitch), :] = piece

    each = 128 // cells
    step = 2 * each
    odd = lax.broadcasted_iota(jnp.int32, (2 * values, 2 * 128), 0) % 2
    position = jnp.concatenate([acquired[...]] * step, axis=1) - odd
    batch = chosen.shape[0] // PARTS
    leaving = []
    for h in range(halves):
        regroup(h)
        for start in range(h * hx, (h + 1) * hx, step):
            pieces = []
            for buffer in (near, far):
                for d in range(-2, 3):
                    for part in range(sets):
                        rows = [(part * xs + x) * pitch + EDGE + d for x in range(start, start + step)]
                        pieces.append(jnp.concatenate([buffer[r : r + cells, :] for r in rows], axis=0).astype(bf16))
            result = nt(weights[...], jnp.concatenate(pieces, axis=1))
            actual = result[6 * values :]
            for ry in range(3):
                estimate = result[ry * 2 * values : (ry + 1) * 2 * values]
                picked = jnp.where(position == 2 * ry, actual, estimate).astype(bf16)
                for half in range(2):
                    at = (start // each + half) * 2 * values
                    chosen[at : at + 2 * values, ry * 128 : (ry + 1) * 128] = picked[:, half * 128 : (half + 1) * 128]
            done = (start + step) // each * 2 * values
            if done % batch == 0:
                part = pl.ds(done - batch, batch)
                leaving.append(pltpu.make_async_copy(chosen.at[part], out.at[part], unload.at[len(leaving)]))
                leaving[-1].start()
    for copy in list(along_x.values()) + list(along_z.values()):
        copy.wait_send()
    for copy in leaving:
        copy.wait()


def spread_kernel(xs, cells, chosen, to_ky, out, chosen_held, to_ky_held, staged, entering, leaving):
    each = 128 // cells
    width = to_ky.shape[1] // each
    batch = chosen.shape[0] // PARTS
    rows = chosen.shape[0] * each // xs
    values = rows // 2
    loading = [pltpu.make_async_copy(to_ky, to_ky_held, entering.at[PARTS])]
    for n in range(PARTS):
        part = pl.ds(n * batch, batch)
        loading.append(pltpu.make_async_copy(chosen.at[part], chosen_held.at[part], entering.at[n]))
    for copy in loading:
        copy.start()
    loading[0].wait()
    stores = []
    for n in range(PARTS):
        loading[n + 1].wait()
        block = chosen_held[n * batch : (n + 1) * batch, :]
        spread = jnp.dot(block, to_ky_held[...], preferred_element_type=jnp.float32).astype(jnp.bfloat16)
        for row in range(0, batch, rows):
            for m in range(each):
                x = (n * batch + row) // rows * each + m
                for s in range(2):
                    first = row + s * values
                    staged[s * xs + x] = spread[first : first + values, m * width : m * width + 3 * cells]
        for s in range(2):
            part = pl.ds(s * xs + n * (xs // PARTS), xs // PARTS)
            stores.append(pltpu.make_async_copy(staged.at[part], out.at[part], leaving.at[len(stores)]))
            stores[-1].start()
    for copy in stores:
        copy.wait()


def local(kspace_lines, acquired_at, ky_start, kz_start, kernels):
    nkz, ngx = lax.axis_size("kz"), lax.axis_size("gx")
    coils, _, own, _, extent = kspace_lines.shape
    xs, cells = extent // ngx, ngx * own
    assert own == GROUP and ngx % 2 == 0 and nkz % GROUP == 0 and 2 * coils * GROUP == 128 and 128 % cells == 0
    each = 128 // cells
    width = -(-3 * cells // 128) * 128
    sets = nkz // GROUP
    halves, hx = 1, xs
    taps = 10 * 128 * sets
    lattice = pltpu.VMEM((sets * xs * (cells + 2 * EDGE), 128), jnp.float32)
    operands = [
        kspace_lines,
        jnp.asarray(line_order(coils, own)),
        jnp.asarray(readout_table(extent).astype(BF16)),
        jnp.transpose(kernels, (0, 1, 3, 2, 4)),
        jnp.asarray(weight_lanes(coils)),
        ky_start,
        kz_start,
        jnp.asarray(row_order(coils)),
        jnp.asarray(slab_order(2 * coils)),
        acquired_at,
    ]
    held = [pltpu.SMEM(o.shape, o.dtype) if o.ndim == 1 else pltpu.VMEM(o.shape, o.dtype) for o in operands]
    chosen = pl.pallas_call(
        functools.partial(kernel, nkz, ngx),
        out_shape=jax.ShapeDtypeStruct((xs // each * 4 * coils, 3 * 128), jnp.bfloat16),
        in_specs=[pl.BlockSpec(memory_space=pltpu.HBM)] * len(operands),
        out_specs=pl.BlockSpec(memory_space=pltpu.HBM),
        scratch_shapes=held + [
            lattice,
            lattice,
            pltpu.VMEM((16 * coils, taps), jnp.bfloat16),
            pltpu.VMEM((nkz, halves, ngx, hx, 128), jnp.bfloat16),
            pltpu.VMEM((ngx, halves, hx, 128), jnp.bfloat16),
            pltpu.VMEM((14 * coils, taps), jnp.bfloat16),
            pltpu.VMEM((xs // each * 4 * coils, 3 * 128), jnp.bfloat16),
            pltpu.SemaphoreType.DMA((len(operands),)),
            pltpu.SemaphoreType.DMA((PARTS,)),
            pltpu.SemaphoreType.DMA((halves, ngx)),
            pltpu.SemaphoreType.DMA((halves, ngx)),
            pltpu.SemaphoreType.DMA((nkz, halves, ngx // 2)),
            pltpu.SemaphoreType.DMA((nkz, halves, ngx // 2)),
        ],
        compiler_params=pltpu.CompilerParams(
            collective_id=0, has_side_effects=True, vmem_limit_bytes=LIMIT),
    )(*operands)
    to_ky = jnp.asarray(lane_order(cells, width))
    hbm = pl.BlockSpec(memory_space=pltpu.HBM)
    filled = pl.pallas_call(
        functools.partial(spread_kernel, xs, cells),
        out_shape=jax.ShapeDtypeStruct((2 * xs, 2 * coils, 3 * cells), jnp.bfloat16),
        in_specs=[hbm, hbm],
        out_specs=hbm,
        scratch_shapes=[
            pltpu.VMEM(chosen.shape, chosen.dtype),
            pltpu.VMEM(to_ky.shape, to_ky.dtype),
            pltpu.VMEM((2 * xs, 2 * coils, 3 * cells), jnp.bfloat16),
            pltpu.SemaphoreType.DMA((PARTS + 1,)),
            pltpu.SemaphoreType.DMA((2 * PARTS,)),
        ],
        compiler_params=pltpu.CompilerParams(vmem_limit_bytes=LIMIT),
    )(chosen, to_ky)
    return filled.reshape(2, xs, coils, 2, 3 * cells)


def solution(mesh):
    placed = (P(None, "kz", "gx", None, None), P("kz", None), P(), P(), P())
    return jax.shard_map(
        local,
        mesh=mesh,
        in_specs=placed,
        out_specs=P(None, "gx", None, "kz", None),
        check_vma=False,
    )
```

```python
import functools
import math

import jax
import jax.numpy as jnp
import ml_dtypes
import numpy as np
from jax import lax
from jax.experimental import pallas as pl
from jax.experimental.pallas import tpu as pltpu
from jax.sharding import PartitionSpec as P

BF16 = ml_dtypes.bfloat16
MESH = pl.DeviceIdType.MESH
GROUP = 4
EDGE = 4
LIMIT = 60 * 1024 * 1024


def readout_table(extent):
    index = np.arange(extent)
    angle = (index[:, None] * index[None, :] % extent) * (2.0 * math.pi / extent)
    return np.concatenate([np.cos(angle), np.sin(angle)], axis=1).astype(np.float64) / math.sqrt(extent)


def line_order(coils, cells):
    order = np.zeros((2, cells, 2, coils, coils, cells, 2), np.float32)
    for c in range(coils):
        for a in range(cells):
            order[0, a, 0, c, c, a, 0] = 1
            order[0, a, 1, c, c, a, 1] = 1
            order[1, a, 0, c, c, a, 1] = -1
            order[1, a, 1, c, c, a, 0] = 1
    return order.reshape(4 * cells * coils, 2 * coils * cells).astype(BF16)


def slab_order(values):
    order = np.zeros((GROUP, GROUP, values, GROUP, GROUP, values), np.float32)
    for b in range(GROUP):
        for a in range(GROUP):
            for v in range(values):
                order[b, a, v, a, b, v] = 1
    return order.reshape(GROUP * GROUP * values, -1).astype(BF16)


def weight_lanes(coils):
    lanes = np.zeros((2, 2, coils, 2, 2, GROUP, 2, coils), np.float32)
    for v in range(2):
        sign = -1 if v else 1
        for c in range(coils):
            lanes[0, v, c, 0, v, :, 0, c] = 1
            lanes[1, v, c, 0, v, :, 1, c] = -sign
            lanes[1, v, c, 1, v, :, 0, c] = 1
            lanes[0, v, c, 1, v, :, 1, c] = sign
    return lanes.reshape(2, 2 * coils, -1).astype(BF16)


def row_order(coils):
    values = 2 * coils
    order = np.zeros((4, values, 2, 7 * values), np.float32)
    for n in range(values):
        for rz in range(2):
            for ry in range(3):
                order[ry, n, rz, (ry * 2 + rz) * values + n] = 1
            order[3, n, rz, 6 * values + n] = 1
    return order.reshape(8 * values, 7 * values).astype(BF16)


def lane_order(cells, width):
    each = 128 // cells
    order = np.zeros((3, each, cells, each, width), np.float32)
    for ry in range(3):
        for x in range(each):
            for a in range(cells):
                order[ry, x, a, x, 3 * a + ry] = 1
    return order.reshape(3 * 128, each * width).astype(BF16)


def nt(left, right):
    return lax.dot_general(left, right, (((1,), (1,)), ((), ())), preferred_element_type=jnp.float32)


def kernel(nkz, ngx, *refs):
    sources, out, held = refs[:11], refs[11], refs[12:23]
    lines, order, table, parts, to_lanes, ky_start, kz_start, to_rows, to_slabs, acquired, to_ky = held
    near, far, weights, planes, spectra, natural, chosen, staged, load, unload, send_x, recv_x, send_z, recv_z = refs[23:]
    b, g = lax.axis_index("kz"), lax.axis_index("gx")
    barrier = pltpu.get_barrier_semaphore()
    for k in range(1, ngx):
        pl.semaphore_signal(barrier, inc=1, device_id=(b, lax.rem(g + k, ngx)), device_id_type=MESH)
    for j in range(1, nkz):
        pl.semaphore_signal(barrier, inc=1, device_id=(lax.rem(b + j, nkz), g), device_id_type=MESH)
    loading = [pltpu.make_async_copy(*pair, load.at[n]) for n, pair in enumerate(zip(sources, held))]
    for copy in loading:
        copy.start()

    f32, bf16 = jnp.float32, jnp.bfloat16
    sets = nkz // GROUP
    coils = parts.shape[3]
    values = 2 * coils
    cells = ngx * GROUP
    pitch = cells + 2 * EDGE
    _, halves, hx, _ = spectra.shape
    xs = halves * hx
    pairs = ngx // 2
    chip, core = g // 2, lax.rem(g, 2)

    count = values * GROUP
    for copy in loading[:2]:
        copy.wait()
    both = jnp.dot(order[...], lines[...].reshape(count, table.shape[0]), preferred_element_type=f32).astype(bf16)
    right = jnp.concatenate([both[:count], both[count:]], axis=1)
    loading[2].wait()
    spectra[...] = nt(table[...], right).astype(bf16).reshape(spectra.shape)
    for h in range(halves):
        planes[b, h, g] = spectra[g, h]

    pl.semaphore_wait(barrier, ngx + nkz - 2)
    along_x, along_z = {}, {}

    def forward(h, m):
        block = planes.at[b, h, pl.ds(2 * lax.rem(chip + pairs - m, pairs), 2)]
        for j in range(1, nkz):
            along_z[j, h, m] = pltpu.make_async_remote_copy(
                src_ref=block, dst_ref=block, send_sem=send_z.at[j, h, m], recv_sem=recv_z.at[j, h, m],
                device_id=(lax.rem(b + j, nkz), g), device_id_type=MESH)
            along_z[j, h, m].start()

    for h in range(halves):
        for k in range(1, ngx):
            to = 2 * lax.rem(chip + k // 2, pairs) + lax.rem(core + k % 2, 2)
            along_x[h, k] = pltpu.make_async_remote_copy(
                src_ref=spectra.at[to, h], dst_ref=planes.at[b, h, g], send_sem=send_x.at[h, k],
                recv_sem=recv_x.at[h, k], device_id=(b, to), device_id_type=MESH)
            along_x[h, k].start()
    along_x[0, 1].wait_recv()
    forward(0, 0)
    for copy in loading[3:]:
        copy.wait()
    terms = (
        jnp.dot(parts[0].reshape(36 * coils, values), to_lanes[0], preferred_element_type=f32)
        + jnp.dot(parts[1].reshape(36 * coils, values), to_lanes[1], preferred_element_type=f32)
    )

    lane = lax.broadcasted_iota(jnp.int32, (coils, 128), 1)
    slab = lane // values

    def place(t):
        here = {n: jnp.full((coils, 128), ky_start[t], jnp.int32) == n for n in (-2, -1, 0)}
        for v in range(2):
            for part in range(sets):
                cell = slab + part * GROUP
                if v:
                    cell = nkz - 1 - cell
                point = cell - b - kz_start[t]
                for s in range(2):
                    column = (s * 2 + v) * 128
                    rows = []
                    for i in range(3):
                        at = (t * 6 + i) * coils
                        first = terms[at : at + coils, column : column + 128]
                        second = terms[at + 3 * coils : at + 4 * coils, column : column + 128]
                        rows.append(jnp.where(point == 0, first, jnp.where(point == 1, second, 0.0)))
                    for d in range(-2, 3):
                        total = jnp.zeros((coils, 128), f32)
                        for i in range(3):
                            if -2 <= d - i <= 0:
                                total = jnp.where(here[d - i], rows[i], total)
                        where = ((v * 5 + d + 2) * sets + part) * 128
                        natural[(t * 2 + s) * coils : (t * 2 + s + 1) * coils, where : where + 128] = total.astype(bf16)

    def place_rest():
        natural[12 * coils :, :] = jnp.zeros((values, natural.shape[1]), bf16)
        row = lax.broadcasted_iota(jnp.int32, (values, 128), 0)
        wide = lax.broadcasted_iota(jnp.int32, (values, 128), 1)
        for part in range(sets):
            same = (b - part * GROUP) * values + row == wide
            where = (2 * sets + part) * 128
            natural[12 * coils :, where : where + 128] = jnp.where(same, 1.0, 0.0).astype(bf16)
        for x in range(sets * xs):
            for buffer in (near, far):
                buffer[x * pitch : x * pitch + EDGE, :] = jnp.zeros((EDGE, 128), f32)
                buffer[(x + 1) * pitch - EDGE : (x + 1) * pitch, :] = jnp.zeros((EDGE, 128), f32)

    work = [functools.partial(place, t) for t in range(6)] + [place_rest]
    for h in range(halves):
        for m in range(pairs):
            if h or m:
                for k in range(max(2 * m, 1), 2 * m + 2):
                    along_x[h, k].wait_recv()
                forward(h, m)
            if work:
                work.pop(0)()
    for piece in work:
        piece()
    weights[...] = jnp.dot(to_rows[...], natural[...], preferred_element_type=f32).astype(bf16)

    def regroup(h):
        for m in range(pairs):
            for j in range(1, nkz):
                along_z[j, h, m].wait_recv()
        for part in range(sets):
            block = jnp.concatenate(
                [planes[part * GROUP + n, h].reshape(ngx * hx, 128) for n in range(GROUP)], axis=1)
            turned = jnp.dot(block, to_slabs[...], preferred_element_type=f32)
            base = (part * xs + h * hx) * pitch + EDGE
            for a in range(cells):
                q, n = a // GROUP, a % GROUP
                piece = turned[q * hx : (q + 1) * hx, n * 128 : (n + 1) * 128]
                near[pl.ds(base + a, hx, stride=pitch), :] = piece
                far[pl.ds(base + cells - 1 - a, hx, stride=pitch), :] = piece

    each = 128 // cells
    width = to_ky.shape[1] // each
    step = 2 * each
    odd = lax.broadcasted_iota(jnp.int32, (2 * values, 2 * 128), 0) % 2
    position = jnp.concatenate([acquired[...]] * step, axis=1) - odd
    batch = chosen.shape[0] // halves
    leaving = []
    for h in range(halves):
        regroup(h)
        for start in range(h * hx, (h + 1) * hx, step):
            pieces = []
            for buffer in (near, far):
                for d in range(-2, 3):
                    for part in range(sets):
                        rows = [(part * xs + x) * pitch + EDGE + d for x in range(start, start + step)]
                        pieces.append(jnp.concatenate([buffer[r : r + cells, :] for r in rows], axis=0).astype(bf16))
            result = nt(weights[...], jnp.concatenate(pieces, axis=1))
            actual = result[6 * values :]
            for ry in range(3):
                estimate = result[ry * 2 * values : (ry + 1) * 2 * values]
                picked = jnp.where(position == 2 * ry, actual, estimate).astype(bf16)
                for half in range(2):
                    at = (start // each + half) * 2 * values
                    chosen[at : at + 2 * values, ry * 128 : (ry + 1) * 128] = picked[:, half * 128 : (half + 1) * 128]
        at = h * batch
        spread = jnp.dot(chosen[at : at + batch, :], to_ky[...], preferred_element_type=f32).astype(bf16)
        for row in range(0, batch, 2 * values):
            for n in range(each):
                x = (at + row) // (2 * values) * each + n
                for s in range(2):
                    first = row + s * values
                    staged[s * xs + x] = spread[first : first + values, n * width : n * width + 3 * cells]
        for s in range(2):
            part = pl.ds(s * xs + h * hx, hx)
            leaving.append(pltpu.make_async_copy(staged.at[part], out.at[part], unload.at[len(leaving)]))
            leaving[-1].start()
    for copy in list(along_x.values()) + list(along_z.values()):
        copy.wait_send()
    for copy in leaving:
        copy.wait()


def copy_kernel(source, target, held, entering, leaving):
    count = entering.shape[0]
    size = source.shape[0] // count
    pairs = []
    for n in range(count):
        part = pl.ds(n * size, size)
        pairs.append((
            pltpu.make_async_copy(source.at[part], held.at[part], entering.at[n]),
            pltpu.make_async_copy(held.at[part], target.at[part], leaving.at[n]),
        ))
    for first, _ in pairs:
        first.start()
    for first, second in pairs:
        first.wait()
        second.start()
    for _, second in pairs:
        second.wait()


def local(kspace_lines, acquired_at, ky_start, kz_start, kernels):
    nkz, ngx = lax.axis_size("kz"), lax.axis_size("gx")
    coils, _, own, _, extent = kspace_lines.shape
    xs, cells = extent // ngx, ngx * own
    assert own == GROUP and ngx % 2 == 0 and nkz % GROUP == 0 and 2 * coils * GROUP == 128 and 128 % cells == 0
    each = 128 // cells
    width = -(-3 * cells // 128) * 128
    sets = nkz // GROUP
    halves = 1
    hx = xs // halves
    taps = 10 * 128 * sets
    lattice = pltpu.VMEM((sets * xs * (cells + 2 * EDGE), 128), jnp.float32)
    operands = [
        kspace_lines,
        jnp.asarray(line_order(coils, own)),
        jnp.asarray(readout_table(extent).astype(BF16)),
        jnp.transpose(kernels, (0, 1, 3, 2, 4)),
        jnp.asarray(weight_lanes(coils)),
        ky_start,
        kz_start,
        jnp.asarray(row_order(coils)),
        jnp.asarray(slab_order(2 * coils)),
        acquired_at,
        jnp.asarray(lane_order(cells, width)),
    ]
    held = [pltpu.SMEM(o.shape, o.dtype) if o.ndim == 1 else pltpu.VMEM(o.shape, o.dtype) for o in operands]
    filled = pl.pallas_call(
        functools.partial(kernel, nkz, ngx),
        out_shape=jax.ShapeDtypeStruct((2 * xs, 2 * coils, 3 * cells), jnp.bfloat16),
        in_specs=[pl.BlockSpec(memory_space=pltpu.HBM)] * len(operands),
        out_specs=pl.BlockSpec(memory_space=pltpu.HBM),
        scratch_shapes=held + [
            lattice,
            lattice,
            pltpu.VMEM((16 * coils, taps), jnp.bfloat16),
            pltpu.VMEM((nkz, halves, ngx, hx, 128), jnp.bfloat16),
            pltpu.VMEM((ngx, halves, hx, 128), jnp.bfloat16),
            pltpu.VMEM((14 * coils, taps), jnp.bfloat16),
            pltpu.VMEM((xs // each * 4 * coils, 3 * 128), jnp.bfloat16),
            pltpu.VMEM((2 * xs, 2 * coils, 3 * cells), jnp.bfloat16),
            pltpu.SemaphoreType.DMA((len(operands),)),
            pltpu.SemaphoreType.DMA((2 * halves,)),
            pltpu.SemaphoreType.DMA((halves, ngx)),
            pltpu.SemaphoreType.DMA((halves, ngx)),
            pltpu.SemaphoreType.DMA((nkz, halves, ngx // 2)),
            pltpu.SemaphoreType.DMA((nkz, halves, ngx // 2)),
        ],
        compiler_params=pltpu.CompilerParams(
            collective_id=0, has_side_effects=True, vmem_limit_bytes=LIMIT),
    )(*operands)
    filled = pl.pallas_call(
        copy_kernel,
        out_shape=jax.ShapeDtypeStruct(filled.shape, filled.dtype),
        in_specs=[pl.BlockSpec(memory_space=pltpu.HBM)],
        out_specs=pl.BlockSpec(memory_space=pltpu.HBM),
        scratch_shapes=[
            pltpu.VMEM(filled.shape, filled.dtype),
            pltpu.SemaphoreType.DMA((8,)),
            pltpu.SemaphoreType.DMA((8,)),
        ],
        compiler_params=pltpu.CompilerParams(vmem_limit_bytes=LIMIT),
    )(filled)
    return filled.reshape(2, xs, coils, 2, 3 * cells)


def solution(mesh):
    placed = (P(None, "kz", "gx", None, None), P("kz", None), P(), P(), P())
    return jax.shard_map(
        local,
        mesh=mesh,
        in_specs=placed,
        out_specs=P(None, "gx", None, "kz", None),
        check_vma=False,
    )
```
